32 devices in a mesh: ctx: 8 (over z, y), grp: 4 (over x, core).
Axes of the slice: x: 2, y: 2, z: 4, core: 2. Of those that a mesh axis runs over, the one named last changes fastest.
Arguments:
- q_nope: bfloat16 [64, 128, 128], P(None, 'ctx'), may hold values from -6 to 6
- q_rope: bfloat16 [64, 128, 64], P(None, 'ctx'), may hold values from -720 to 720
- w_uk: bfloat16 [128, 128, 512], P('ctx'), may hold values from -0.5 to 0.5
- w_uv: bfloat16 [128, 512, 128], P('ctx'), may hold values from -0.375 to 0.375
- prompt: bfloat16 [1536, 576], P('grp'), may hold values from -12 to 12
- w_out: bfloat16 [16384, 7168], P('ctx', 'grp'), may hold values from -0.0625 to 0.0625
- residual: bfloat16 [64, 7168], P('ctx', 'grp'), may hold values from -3 to 3
- routes: int32 [64, 8], P('ctx'), may hold values from 0 to 31, all different within a row; in each aligned block of 8 rows (0 to 7, 8 to 15, ...) at most 4 rows name the same one
- route_scores: float32 [64, 8], P('ctx'), may hold values from 0.05 to 1
- expert_gate: bfloat16 [32, 7168, 1024], P('ctx', 'grp'), may hold values from -0.0625 to 0.0625
- expert_up: bfloat16 [32, 7168, 1024], P('ctx', 'grp'), may hold values from -0.0625 to 0.0625
- expert_down: bfloat16 [32, 1024, 7168], P('ctx', None, 'grp'), may hold values from -0.1875 to 0.1875
Outputs:
- layer_out: bfloat16 [64, 7168], P('ctx', 'grp')
The draws below stay inside these ranges and needn't reach their ends.
Inputs may be any that keep to these rules, and one draw needn't show every extreme that they name: `routes`: in each aligned block of 8 rows no expert is named by more than 4 rows, a bound that some block reaches; the 8 experts of a row differ.
All inputs are finite; a program needn't handle non-finite values.
Results may differ from the reference program's by a relative error of at most 0.0163.
Values may be sent and summed in bfloat16 or wider, within the bound.
No kernel may reach another device: no remote copies, remote signals or barrier semaphores. Data moves between devices by JAX's collectives and lax.ppermute only.
A program may use at most 128 MiB of HBM per device.

```python
import math
import jax
import jax.numpy as jnp
import numpy as np
from jax import lax

D = 7168
H = 128
NOPE = 128
ROPE = 64
LAT = 512
VDIM = 128
TOPK = 8
FF = 1024
ROW_DEV = 8
EXPERTS = 32
CAP = 4
ROWS = 64
PROMPT = 1536


def prompt_table(key):
    base_key = jax.random.fold_in(key, 11)
    first_key = jax.random.fold_in(base_key, 0)
    table = jnp.clip(jax.random.normal(first_key, (PROMPT, LAT + ROPE), jnp.float32), -6.0, 6.0)
    return table


def draw_prompt(key, part):
    return prompt_table(key).astype(jnp.bfloat16)


def draw_q_rope(key, part):
    first_key = jax.random.fold_in(jax.random.fold_in(key, 23), 0)
    noise = jnp.clip(jax.random.normal(first_key, (ROWS, H, ROPE), jnp.float32), -6.0, 6.0)
    return noise.astype(jnp.bfloat16)


def block_levels(stream_key, shape, pieces, least, largest):
    def one(position, parts):
        draws = jax.random.uniform(jax.random.fold_in(jax.random.fold_in(stream_key, 6), position), (parts,), jnp.float32, least / len(pieces), largest / len(pieces))
        return jnp.repeat(jnp.exp(draws), shape[position] // parts).reshape((-1,) + (1,) * (len(shape) - position - 1))

    factor_of = one(*pieces[0])
    for cut in pieces[1:]:
        factor_of = factor_of * one(*cut)
    return factor_of


def assign_block(stream_key, own, number, rows, number_of, top, most, lean):
    sequence = jax.random.permutation(stream_key, number_of)
    heavy_load, common = portions_of(number_of, rows * top, most, lean, True), portions_of(number_of, rows * top, most, lean, False)
    places = jnp.arange(number_of)

    def named(sizes, turn):
        used = int((sizes > 0).sum())
        fixed = max(1, used // 4)
        moved = fixed + (places - fixed + turn * (used - fixed)) % max(1, number_of - fixed)
        return jnp.zeros((number_of,), jnp.int32).at[sequence[jnp.where(places < fixed, places, moved)]].set(jnp.asarray(sizes, jnp.int32))

    sizes = jnp.where(number % 4 == 0, named(heavy_load, number // 4), named(common, number - number // 4 - 1))
    mixed = jax.random.permutation(jax.random.fold_in(own, 3), number_of)
    donor, receiver = mixed[0:number_of // 2 * 2:2], mixed[1:number_of // 2 * 2:2]
    room = jnp.minimum(sizes[donor] - 1, most - sizes[receiver]) // 2
    room = jnp.where((donor == sequence[0]) | (receiver == sequence[0]) | (sizes[receiver] == 0), 0, jnp.maximum(room, 0))
    moved = jax.random.randint(jax.random.fold_in(own, 4), (number_of // 2,), 0, 1 << 20) % (room + 1)
    sizes = sizes.at[donor].add(-moved).at[receiver].add(moved)
    items = jnp.searchsorted(jnp.cumsum(sizes), jnp.arange(rows * top), side="right").astype(jnp.int32)
    grid = items.reshape(top, rows).T
    grid = grid[jax.random.permutation(jax.random.fold_in(own, 1), rows)]
    turn = jax.random.randint(jax.random.fold_in(own, 2), (rows, 1), 0, top)
    return jnp.take_along_axis(grid, (jnp.arange(top)[None, :] + turn) % top, axis=1)


def portions_of(number_of, total, limit, skew, full):
    weights = [(1 << 20) // math.isqrt(standing ** skew) + 1 for standing in range(1, number_of + 1)]
    largest = limit if full else min(limit, max(-(-total // number_of), total * weights[0] // sum(weights)))
    least = 1 if total - largest >= number_of - 1 else 0
    counts, surplus = [largest] + [least] * (number_of - 1), total - largest - least * (number_of - 1)
    while surplus > 0:
        movable = [i for i in range(1, number_of) if counts[i] < largest] or [i for i in range(1, number_of) if counts[i] < limit]
        pool, remaining = sum([weights[i] for i in movable]), surplus
        for i in movable:
            more = min(limit - counts[i], max(1, remaining * weights[i] // pool), surplus)
            counts[i] = counts[i] + more
            surplus = surplus - more
    return np.array(counts)


def bell_draw(stream_key, extent, spread, reach, pieces=(), held_as=jnp.bfloat16):
    values = jax.random.normal(stream_key, extent, jnp.float32) * spread
    if len(pieces) > 0:
        values = block_levels(stream_key, extent, pieces, -0.22, 0.18) * values
    return jnp.clip(values, min=-reach, max=reach).astype(held_as)


def setup_inputs(seed: int = 0) -> dict:
    streams_of = jax.random.split(jax.random.key(seed), 13)
    q_nope = bell_draw(streams_of[0], (ROWS, H, NOPE), 1.0, 6.0, ((1, 8),))
    q_rope = draw_q_rope(jax.random.fold_in(streams_of[12], 71), 0)
    w_uk = bell_draw(streams_of[2], (H, NOPE, LAT), NOPE ** -0.5, 0.5, ((0, 8),))
    w_uv = bell_draw(streams_of[3], (H, LAT, VDIM), (LAT // 2) ** -0.5, 0.375, ((0, 8),))
    prompt = draw_prompt(jax.random.fold_in(streams_of[12], 71), 0)
    w_out = bell_draw(streams_of[5], (H * VDIM, D), (H * VDIM // 2) ** -0.5, 0.0625, ((0, 8), (1, 4)))
    residual = bell_draw(streams_of[6], (ROWS, D), 0.5, 3.0, ((0, 8), (1, 4)))
    routes_keys = jax.random.split(jax.random.fold_in(streams_of[7], 1), ROWS // ROW_DEV)
    routes_turns = jax.random.permutation(jax.random.fold_in(streams_of[7], 3), ROWS // ROW_DEV)
    routes = jax.vmap(lambda own, number: assign_block(jax.random.fold_in(streams_of[7], 2), own, number, ROW_DEV, EXPERTS, TOPK, CAP, 2))(routes_keys, routes_turns).reshape((ROWS, TOPK))
    route_scores = jnp.clip(0.05 + 0.95 * jax.random.uniform(streams_of[8], (ROWS, TOPK), jnp.float32) ** block_levels(streams_of[8], (ROWS, TOPK), ((0, 8),), -0.2, 0.2), 0.05, 1.0)
    expert_gate = bell_draw(streams_of[9], (EXPERTS, D, FF), D ** -0.5, 0.0625, ((0, 8), (1, 4)))
    expert_up = bell_draw(streams_of[10], (EXPERTS, D, FF), D ** -0.5, 0.0625, ((0, 8), (1, 4)))
    expert_down = bell_draw(streams_of[11], (EXPERTS, FF, D), FF ** -0.5, 0.1875, ((0, 8), (2, 4)))
    return {"q_nope": q_nope, "q_rope": q_rope, "w_uk": w_uk, "w_uv": w_uv, "prompt": prompt, "w_out": w_out, "residual": residual, "routes": routes, "route_scores": route_scores, "expert_gate": expert_gate, "expert_up": expert_up, "expert_down": expert_down}


route_factor = 2.5


def reference(q_nope, q_rope, w_uk, w_uv, prompt, w_out, residual, routes, route_scores, expert_gate, expert_up, expert_down):
    score_scale = (NOPE + ROPE) ** -0.5
    q_latent = jnp.einsum("rhn,hnl->rhl", q_nope.astype(jnp.float32), w_uk.astype(jnp.float32)).astype(jnp.bfloat16)
    queries = jnp.concatenate([q_latent, q_rope], axis=-1)
    latents = prompt[:, :LAT]

    def one_head(packed):
        head_query, head_uv = packed
        scores = jnp.dot(head_query, prompt.T, preferred_element_type=jnp.float32) * score_scale
        top_score = jnp.max(scores, axis=-1, keepdims=True)
        raised = jnp.exp(scores - top_score)
        denominator = jnp.sum(raised, axis=-1, keepdims=True)
        weighted = jnp.dot(raised.astype(jnp.bfloat16), latents, preferred_element_type=jnp.float32)
        values = jnp.dot(weighted, head_uv.astype(jnp.float32), precision=lax.Precision.HIGHEST)
        return (values / denominator).astype(jnp.bfloat16)

    heads_out = lax.map(one_head, (jnp.transpose(queries, (1, 0, 2)), w_uv))
    attended = jnp.transpose(heads_out, (1, 0, 2)).reshape(ROWS, H * VDIM)
    hidden = residual.astype(jnp.float32) + jnp.dot(attended, w_out, preferred_element_type=jnp.float32)
    moe_input = hidden.astype(jnp.bfloat16)
    gate_weights = route_factor * route_scores / jnp.sum(route_scores, axis=-1, keepdims=True)

    def one_expert(running, packed):
        expert_index, w_gate, w_up, w_down = packed
        row_weight = jnp.sum(jnp.where(routes == expert_index, gate_weights, 0.0), axis=-1)
        gate_sum = jnp.dot(moe_input, w_gate, preferred_element_type=jnp.float32)
        up_sum = jnp.dot(moe_input, w_up, preferred_element_type=jnp.float32)
        activated = (jax.nn.silu(gate_sum) * up_sum).astype(jnp.bfloat16)
        result = jnp.dot(activated, w_down, preferred_element_type=jnp.float32).astype(jnp.bfloat16)
        return running + row_weight[:, None] * result.astype(jnp.float32), None

    expert_ids = jnp.arange(EXPERTS, dtype=jnp.int32)
    combined = lax.scan(one_expert, jnp.zeros((ROWS, D), jnp.float32), (expert_ids, expert_gate, expert_up, expert_down))[0]
    return (hidden + combined).astype(jnp.bfloat16)
```

```python
import jax
import jax.numpy as jnp
from jax import lax
from jax.sharding import PartitionSpec as P

LAT = 512
CAP = 4
route_factor = 2.5
F32 = jnp.float32
BF16 = jnp.bfloat16


def swap(x, axis, bits):
    size = lax.axis_size(axis)
    return lax.ppermute(x, axis, [(a, a ^ bits) for a in range(size)])


def pick(x, index, axis=0):
    return lax.dynamic_index_in_dim(x, index, axis, keepdims=False)


def ctx_scatter_sum(x):
    size = lax.axis_size("ctx")
    me = lax.axis_index("ctx")
    low, high = me & 1, me >> 1
    x = x.reshape(size // 2, 2, -1, x.shape[-1])
    got = swap(pick(x, 1 - low, 1).astype(BF16), "ctx", 1)
    x = pick(x, low, 1) + got.astype(F32)
    total = pick(x, high)
    sends = [pick(x, high ^ s).astype(BF16) for s in range(1, size // 2)]
    for s, part in enumerate(sends, 1):
        total = total + swap(part, "ctx", 2 * s).astype(F32)
    return total


def ctx_gather(x):
    size = lax.axis_size("ctx")
    me = lax.axis_index("ctx")
    low, high = me & 1, me >> 1
    parts = [x] + [swap(x, "ctx", 2 * s) for s in range(1, size // 2)]
    mine = jnp.stack(parts)
    other = swap(mine, "ctx", 1)
    both = jnp.stack([jnp.where(low == 0, mine, other), jnp.where(low == 0, other, mine)], 1)
    order = jnp.arange(size // 2) ^ high
    pickm = (order[:, None] == jnp.arange(size // 2)[None, :]).astype(x.dtype)
    rows = both.shape[2]
    out = jnp.dot(pickm, both.reshape(size // 2, -1), precision=lax.Precision.HIGHEST if x.dtype == F32 else None, preferred_element_type=F32).astype(x.dtype)
    return out.reshape(size * rows, x.shape[1])


def per_device(
    q_nope, q_rope, w_uk, w_uv, prompt, w_out, residual, routes, route_scores,
    expert_gate, expert_up, expert_down,
):
    rows, heads, nope = q_nope.shape
    vdim = w_uv.shape[2]
    score_scale = (nope + q_rope.shape[2]) ** (-0.5)
    grp_size = lax.axis_size("grp")
    ctx_size = lax.axis_size("ctx")
    core = lax.axis_index("grp") & 1
    ctx = lax.axis_index("ctx")
    gate_weights = route_factor * route_scores / jnp.sum(route_scores, axis=-1, keepdims=True)
    info = ctx_gather(jnp.concatenate([routes.astype(F32), gate_weights], axis=1))
    all_routes = info[:, : routes.shape[1]].astype(jnp.int32)
    all_weights = info[:, routes.shape[1] :]
    local_experts = expert_gate.shape[0]
    local_rows = residual.shape[0]
    cap = CAP * ctx_size
    expert_ids = ctx * local_experts + jnp.arange(local_experts)
    named = all_routes[None] == expert_ids[:, None, None]
    hit = jnp.any(named, -1)
    weight = jnp.sum(jnp.where(named, all_weights[None], 0.0), -1)
    blocks = hit.reshape(local_experts, ctx_size, local_rows).astype(jnp.int32)
    rank = (jnp.cumsum(blocks, -1) - blocks).reshape(local_experts, rows)
    slot = (jnp.arange(rows) // local_rows)[None] * CAP + rank
    select = hit[:, None, :] & (slot[:, None, :] == jnp.arange(cap)[None, :, None])
    q_latent = jnp.einsum("rhn,hnl->hrl", q_nope, w_uk, preferred_element_type=F32).astype(BF16)
    queries = jnp.concatenate([q_latent, jnp.transpose(q_rope, (1, 0, 2))], axis=-1)
    scores = jnp.einsum("hrc,jc->hrj", queries, prompt, preferred_element_type=F32) * score_scale
    top = jnp.max(scores, axis=-1)
    raised = jnp.exp(scores - top[..., None])
    total = jnp.sum(raised, axis=-1)
    weighted = jnp.einsum(
        "hrj,jl->hrl", raised.astype(BF16), prompt[:, :LAT], preferred_element_type=F32
    )
    values = jnp.einsum(
        "hrl,hlv->rhv", weighted, w_uv.astype(F32), precision=lax.Precision.HIGHEST
    )
    values = values / total.T[..., None]
    lse = (top + jnp.log(total)).T
    half = rows // 2
    mine_v = lax.dynamic_slice_in_dim(values, core * half, half, 0)
    mine_l = lax.dynamic_slice_in_dim(lse, core * half, half, 0)
    send_v = lax.dynamic_slice_in_dim(values, (1 - core) * half, half, 0).astype(BF16)
    send_l = lax.dynamic_slice_in_dim(lse, (1 - core) * half, half, 0)

    def merge(vs, ls):
        ls = jnp.stack(ls)
        m = jnp.max(ls, 0)
        w = jnp.exp(ls - m)
        tot = jnp.sum(w, 0)
        w = w / tot
        out = sum(w[i][..., None] * v.astype(F32) for i, v in enumerate(vs))
        return out, m + jnp.log(tot)

    v, l = merge([mine_v, swap(send_v, "grp", 1)], [mine_l, swap(send_l, "grp", 1)])
    vb = v.astype(BF16)
    v, l = merge(
        [v] + [swap(vb, "grp", 2 * s) for s in range(1, grp_size // 2)],
        [l] + [swap(l, "grp", 2 * s) for s in range(1, grp_size // 2)],
    )
    mine = v.astype(BF16).reshape(half, heads * vdim)
    other = swap(mine, "grp", 1)
    attended = jnp.concatenate(
        [jnp.where(core == 0, mine, other), jnp.where(core == 0, other, mine)], 0
    )
    projected = ctx_scatter_sum(jnp.dot(attended, w_out, preferred_element_type=F32))
    hidden = residual.astype(F32) + projected
    moe_input = ctx_gather(hidden.astype(BF16))
    selb = select.astype(BF16).reshape(local_experts * cap, rows)
    arrived = jnp.dot(selb, moe_input, preferred_element_type=F32).astype(BF16)
    arrived = arrived.reshape(local_experts, cap, -1)
    ff = expert_gate.shape[2]
    gate = jnp.einsum("esd,edf->esf", arrived, expert_gate, preferred_element_type=F32)
    up = jnp.einsum("esd,edf->esf", arrived, expert_up, preferred_element_type=F32)

    def cut(x, c):
        return lax.dynamic_slice_in_dim(x, c * (ff // 2), ff // 2, 2)

    got = swap(jnp.stack([cut(gate, 1 - core), cut(up, 1 - core)]).astype(BF16), "grp", 1)
    part = jnp.stack([cut(gate, core), cut(up, core)]) + got.astype(F32)
    partb = part.astype(BF16)
    for s in range(1, grp_size // 2):
        part = part + swap(partb, "grp", 2 * s).astype(F32)
    act = (jax.nn.silu(part[0]) * part[1]).astype(BF16)
    act_other = swap(act, "grp", 1)
    activated = jnp.concatenate(
        [jnp.where(core == 0, act, act_other), jnp.where(core == 0, act_other, act)], 2
    )
    result = jnp.einsum(
        "esf,efd->esd", activated, expert_down, preferred_element_type=F32
    ).astype(BF16)
    mix = (select * weight[:, None, :]).astype(F32).reshape(local_experts * cap, rows)
    combined = jnp.einsum(
        "sr,sd->rd", mix, result.reshape(local_experts * cap, -1).astype(F32),
        precision=lax.Precision.HIGHEST,
    )
    return (hidden + ctx_scatter_sum(combined)).astype(BF16)


def solution(mesh):
    in_specs = (
        P(None, "ctx", None),
        P(None, "ctx", None),
        P("ctx", None, None),
        P("ctx", None, None),
        P("grp", None),
        P("ctx", "grp"),
        P("ctx", "grp"),
        P("ctx", None),
        P("ctx", None),
        P("ctx", "grp", None),
        P("ctx", "grp", None),
        P("ctx", None, "grp"),
    )
    return jax.shard_map(
        per_device, mesh=mesh, in_specs=in_specs, out_specs=P("ctx", "grp"), check_vma=False
    )
```

```python
import jax
import jax.numpy as jnp
from jax import lax
from jax.experimental import pallas as pl
from jax.experimental.pallas import tpu as pltpu
from jax.sharding import PartitionSpec as P

CAP = 4
LANES = 128
route_factor = 2.5
F32 = jnp.float32
BF16 = jnp.bfloat16
VMEM = pltpu.VMEM


def swap(x, axis, bits):
    return lax.ppermute(x, axis, [(a, a ^ bits) for a in range(lax.axis_size(axis))])


def spread(x, axis):
    return [swap(x, axis, 2 * s) for s in range(1, lax.axis_size(axis) // 2)]


def run(name, body, outs, ins, scratch=(), us=1.0, limit=8, hbm=()):
    ins = [
        pltpu.with_memory_space_constraint(a, pltpu.HBM) if i in hbm else a
        for i, a in enumerate(ins)
    ]
    return pl.pallas_call(
        body,
        out_shape=[jax.ShapeDtypeStruct(s, d) for s, d in outs],
        in_specs=[
            pl.BlockSpec(memory_space=pltpu.HBM if i in hbm else VMEM) for i in range(len(ins))
        ],
        out_specs=[pl.BlockSpec(memory_space=VMEM) for _ in outs],
        scratch_shapes=list(scratch),
        cost_estimate=pl.CostEstimate(
            flops=int(us * 1.15e9), bytes_accessed=1024, transcendentals=0
        ),
        compiler_params=pltpu.CompilerParams(vmem_limit_bytes=limit << 20),
        name=name,
    )(*ins)


def split3(x):
    hi = x.astype(BF16).astype(F32)
    mid = (x - hi).astype(BF16).astype(F32)
    return hi, mid, x - hi - mid


def pack_lse(x, heads):
    hi, mid, lo = split3(x)
    return (hi + pltpu.roll(mid, heads, 1) + pltpu.roll(lo, 2 * heads, 1)).astype(BF16)


def unpack_lse(x, heads):
    x = x.astype(F32)
    x = x + pltpu.roll(x, LANES - heads, 1) + pltpu.roll(x, LANES - 2 * heads, 1)
    lane = lax.broadcasted_iota(jnp.int32, x.shape, 1)
    return jnp.where(lane < heads, x, 0.0)


def attend_body(qn_h, qr_h, wuk_h, wuv_h, prompt_h, keep, send, qn, qr, wuk, wuv, prompt, rows_scr, sems):
    rows, heads, nope = qn.shape
    lat, vdim = wuk.shape[2], wuv.shape[2]
    half, width = rows // 2, heads * vdim
    group = min(4, heads)
    steps = heads // group
    core = lax.axis_index("grp") & 1
    copies = [
        pltpu.make_async_copy(qn_h, qn, sems.at[0]),
        pltpu.make_async_copy(qr_h, qr, sems.at[1]),
        pltpu.make_async_copy(prompt_h, prompt, sems.at[2]),
    ]
    uk = [
        pltpu.make_async_copy(
            wuk_h.at[pl.ds(c * group, group)], wuk.at[pl.ds(c * group, group)], sems.at[3 + c]
        )
        for c in range(steps)
    ]
    uv = [
        pltpu.make_async_copy(
            wuv_h.at[pl.ds(c * group, group)], wuv.at[pl.ds(c * group, group)], sems.at[3 + steps + c]
        )
        for c in range(steps)
    ]
    copies[0].start()
    uk[0].start()
    copies[1].start()
    copies[2].start()
    for c in range(steps):
        if c:
            uk[c].start()
        uv[c].start()
    scale = (nope + qr.shape[2]) ** (-0.5)
    copies[0].wait()
    queries = jnp.swapaxes(qn[...], 0, 1)
    copies[1].wait()
    turned = jnp.swapaxes(qr[...], 0, 1)
    lane = lax.broadcasted_iota(jnp.int32, (rows, LANES), 1)
    lse = jnp.zeros((rows, LANES), F32)
    for c in range(steps):
        own = range(c * group, (c + 1) * group)
        uk[c].wait()
        q = jnp.concatenate(
            [jnp.dot(queries[h], wuk[h], preferred_element_type=F32).astype(BF16) for h in own], 0
        )
        r = jnp.concatenate([turned[h] for h in own], 0)
        if c == 0:
            copies[2].wait()
        s = jnp.dot(q, prompt[:lat], preferred_element_type=F32)
        s = (s + jnp.dot(r, prompt[lat:], preferred_element_type=F32)) * scale
        top = jnp.max(s, -1, keepdims=True)
        p = jnp.exp(s - top)
        total = jnp.sum(p, -1, keepdims=True)
        w = lax.dot_general(
            p.astype(BF16), prompt[:lat], (((1,), (1,)), ((), ())), preferred_element_type=F32
        )
        w = w * (1.0 / total)
        hi = w.astype(BF16)
        lo = (w - hi.astype(F32)).astype(BF16)
        part = top + jnp.log(total)
        uv[c].wait()
        for i, h in enumerate(own):
            at = slice(i * rows, (i + 1) * rows)
            v = jnp.dot(jnp.concatenate([hi[at], lo[at]], 0), wuv[h], preferred_element_type=F32)
            rows_scr[:, h * vdim : (h + 1) * vdim] = v[:rows] + v[rows:]
            lse = jnp.where(lane == h, part[at], lse)
    rows_scr[:, width:] = lse
    keep[...] = rows_scr[pl.ds(pl.multiple_of(core * half, half), half)]
    out = rows_scr[pl.ds(pl.multiple_of((1 - core) * half, half), half)]
    send[:, :width] = out[:, :width].astype(BF16)
    send[:, width:] = pack_lse(out[:, width:], heads)


def merge_values(heads, own, others):
    width = own.shape[1] - LANES
    vdim = width // heads
    levels = [own[:, width:]] + [unpack_lse(o[:, width:], heads) for o in others]
    top = levels[0]
    for x in levels[1:]:
        top = jnp.maximum(top, x)
    raised = [jnp.exp(x - top) for x in levels]
    total = sum(raised)
    shares = [x / total for x in raised]
    cols = []
    for h in range(heads):
        at = slice(h * vdim, (h + 1) * vdim)
        v = own[:, at] * shares[0][:, h : h + 1]
        for share, o in zip(shares[1:], others):
            v = v + o[:, at].astype(F32) * share[:, h : h + 1]
        cols.append(v)
    lane = lax.broadcasted_iota(jnp.int32, top.shape, 1)
    return cols, jnp.where(lane < heads, top + jnp.log(total), 0.0)


def pair_body(heads, own, other, keep, send):
    width = own.shape[1] - LANES
    vdim = width // heads
    cols, lse = merge_values(heads, own, [other])
    for h, v in enumerate(cols):
        keep[:, h * vdim : (h + 1) * vdim] = v
        send[:, h * vdim : (h + 1) * vdim] = v.astype(BF16)
    keep[:, width:] = lse
    send[:, width:] = pack_lse(lse, heads)


def final_body(heads, own, *refs):
    out = refs[-1]
    vdim = (own.shape[1] - LANES) // heads
    cols, _ = merge_values(heads, own, refs[:-1])
    for h, v in enumerate(cols):
        out[:, h * vdim : (h + 1) * vdim] = v.astype(BF16)


def place(ctx, turn, s):
    return ctx ^ (2 * s + turn)


def store_blocks(ref, blocks, width):
    step = 16 // blocks[0].shape[0]
    for i in range(0, len(blocks), step):
        part = jnp.concatenate(blocks[i : i + step], 0).astype(BF16)
        n = blocks[0].shape[0]
        ref[i * n : (i + step) * n, :width] = part


def project_body(mine, other, routes, scores, w, keep, send, info, att, res, pad):
    half = mine.shape[0]
    width = w.shape[1]
    tail = send.shape[1] - LANES
    count, top = routes.shape
    n = keep.shape[0] // count
    core = lax.axis_index("grp") & 1
    ctx = lax.axis_index("ctx")
    att[pl.ds(pl.multiple_of(core * half, half), half)] = mine[...]
    att[pl.ds(pl.multiple_of((1 - core) * half, half), half)] = other[...]
    res[...] = jnp.dot(att[...], w[...], preferred_element_type=F32)

    def block(turn, s):
        return res[pl.ds(pl.multiple_of(place(ctx, turn, s) * count, count), count)]

    store_blocks(send, [block(1, s) for s in range(n)], width)
    for s in range(n):
        keep[s * count : (s + 1) * count] = block(0, s)
    v = scores[...]
    v = route_factor * v / jnp.sum(v, -1, keepdims=True)
    hi, mid, lo = split3(v)
    pad[...] = jnp.zeros_like(pad)
    for i, x in enumerate((routes[...].astype(F32), hi, mid, lo)):
        pad[:count, i * top : (i + 1) * top] = x
    if tail > width:
        send[:, width:tail] = jnp.zeros((send.shape[0], tail - width), BF16)
    send[:, tail:] = jnp.zeros((send.shape[0], LANES), BF16)
    send[: pad.shape[0], tail:] = pad[...].astype(BF16)
    info[...] = pad[:count]


def pair_rows_body(has_info, *refs):
    keep, other = refs[:2]
    if has_info:
        info, own, *sends, info2 = refs[2:]
    else:
        own, *sends = refs[2:]
    count, width = own.shape
    tail = other.shape[1] - LANES
    if has_info:
        theirs = other[:16, tail:].astype(F32)[:count]
        both = info[...] + pltpu.roll(theirs, 64, 1)
        info2[...] = both
    for s in range(len(sends) + 1):
        if s % 2 == 0:
            pair = other[s * count : (s + 2) * count, :width].astype(F32)
        x = keep[s * count : (s + 1) * count] + pair[(s % 2) * count : (s % 2 + 1) * count]
        if s == 0:
            own[...] = x
        else:
            sends[s - 1][:, :width] = x.astype(BF16)
            if has_info:
                if tail > width:
                    sends[s - 1][:, width:tail] = jnp.zeros((count, tail - width), BF16)
                sends[s - 1][:, tail:] = both.astype(BF16)


def hidden_body(own, residual, *refs):
    *others, hidden, moe = refs
    width = own.shape[1]
    x = own[...] + residual[...].astype(F32)
    for o in others:
        x = x + o[:, :width].astype(F32)
    hidden[...] = x
    moe[...] = x.astype(BF16)


def route_body(local_experts, top, info, *refs):
    *others, pick, mix = refs
    count = info.shape[0]
    ctx = lax.axis_index("ctx")
    blocks = [info[...]] + [o[:, o.shape[1] - LANES :].astype(F32) for o in others]
    near = jnp.concatenate(blocks, 0)
    table = jnp.concatenate([near, pltpu.roll(near, 64, 1)], 0)
    rows = table.shape[0]
    weights = (
        pltpu.roll(table, LANES - top, 1)
        + pltpu.roll(table, LANES - 2 * top, 1)
        + pltpu.roll(table, LANES - 3 * top, 1)
    )
    lane = lax.broadcasted_iota(jnp.int32, (rows, LANES), 1)
    hits, gains = [], []
    all_hits = jnp.zeros((rows, LANES), F32)
    for e in range(local_experts):
        named = (table == (ctx * local_experts + e).astype(F32)) & (lane < top)
        hit = jnp.sum(jnp.where(named, 1.0, 0.0), -1, keepdims=True)
        gains.append(jnp.sum(jnp.where(named, weights, 0.0), -1, keepdims=True))
        hits.append(hit)
        all_hits = jnp.where(lane == e, hit, all_hits)
    a = lax.broadcasted_iota(jnp.int32, (rows, rows), 0)
    b = lax.broadcasted_iota(jnp.int32, (rows, rows), 1)
    earlier = jnp.where((a // count == b // count) & (b < a), 1.0, 0.0).astype(BF16)
    rank = jnp.dot(earlier, all_hits.astype(BF16), preferred_element_type=F32)
    slots = mix.shape[1]
    cap = slots // local_experts
    wide = lax.broadcasted_iota(jnp.int32, (rows, slots), 1)
    start = lax.broadcasted_iota(jnp.int32, (rows, 1), 0) // count * CAP
    chosen = jnp.zeros((rows, slots), F32)
    gain = jnp.zeros((rows, slots), F32)
    for e in range(local_experts):
        slot = rank[:, e : e + 1].astype(jnp.int32) + start + e * cap
        at = (wide == slot) & (hits[e] > 0.5)
        chosen = jnp.where(at, 1.0, chosen)
        gain = jnp.where(at, gains[e], gain)
    pick[...] = jnp.transpose(chosen).astype(BF16)
    mix[...] = gain


def rows_body(*refs):
    *parts, out = refs
    width = out.shape[1]
    store_blocks(out, [p[...].astype(F32) for p in parts], width)


def first_half_body(experts, pick, near, far, gate, up, *refs):
    *maybe, send = refs
    hid = send.shape[2] // 2
    cap = send.shape[1]
    core = lax.axis_index("grp") & 1
    cols = pl.ds(pl.multiple_of((1 - core) * hid, hid), hid)
    rows = jnp.concatenate([near[...], far[...]], 0)
    x = jnp.dot(pick[...], rows, preferred_element_type=F32).astype(BF16)
    maybe[0][...] = x
    for i, e in enumerate(experts):
        xe = x[e * cap : (e + 1) * cap]
        send[i, :, :hid] = jnp.dot(xe, gate[e, :, cols], preferred_element_type=F32).astype(BF16)
        send[i, :, hid:] = jnp.dot(xe, up[e, :, cols], preferred_element_type=F32).astype(BF16)


def next_half_body(experts, x, gate, up, send):
    hid = send.shape[2] // 2
    cap = send.shape[1]
    core = lax.axis_index("grp") & 1
    cols = pl.ds(pl.multiple_of((1 - core) * hid, hid), hid)
    for i, e in enumerate(experts):
        xe = x[e * cap : (e + 1) * cap]
        send[i, :, :hid] = jnp.dot(xe, gate[e, :, cols], preferred_element_type=F32).astype(BF16)
        send[i, :, hid:] = jnp.dot(xe, up[e, :, cols], preferred_element_type=F32).astype(BF16)


def own_half_body(experts, x, gate, up, other, keep, send):
    hid = send.shape[2] // 2
    cap = send.shape[1]
    core = lax.axis_index("grp") & 1
    cols = pl.ds(pl.multiple_of(core * hid, hid), hid)
    for i, e in enumerate(experts):
        xe = x[e * cap : (e + 1) * cap]
        for j, w in enumerate((gate, up)):
            at = slice(j * hid, (j + 1) * hid)
            v = jnp.dot(xe, w[e, :, cols], preferred_element_type=F32)
            v = v + other[i, :, at].astype(F32)
            keep[i, :, at] = v
            send[i, :, at] = v.astype(BF16)


def act_body(keep, *refs):
    *others, out = refs
    hid = out.shape[2]
    for i in range(out.shape[0]):
        x = keep[i]
        for o in others:
            x = x + o[i].astype(F32)
        gate, up = x[:, :hid], x[:, hid:]
        out[i] = (gate / (1.0 + jnp.exp(-gate)) * up).astype(BF16)


def down_body(experts, last, mine, other, down, mix, *refs):
    hid = mine.shape[2]
    cap = mine.shape[1]
    core = lax.axis_index("grp") & 1
    low = pl.ds(pl.multiple_of(core * hid, hid), hid)
    high = pl.ds(pl.multiple_of((1 - core) * hid, hid), hid)
    parts = []
    for i, e in enumerate(experts):
        v = jnp.dot(mine[i], down[e, low], preferred_element_type=F32)
        v = v + jnp.dot(other[i], down[e, high], preferred_element_type=F32)
        parts.append(v.astype(BF16))
    result = jnp.concatenate(parts, 0)
    gain = mix[:, experts[0] * cap : (experts[-1] + 1) * cap]
    hi = gain.astype(BF16)
    lo = (gain - hi.astype(F32)).astype(BF16)
    v = jnp.dot(hi, result, preferred_element_type=F32)
    v = v + jnp.dot(lo, result, preferred_element_type=F32)
    if experts[0]:
        v = v + refs[0][...]
    if not last:
        refs[-1][...] = v
    else:
        keep, send = refs[-2:]
        half = keep.shape[0]
        keep[...] = v[:half]
        send[...] = v[half:].astype(BF16)


def out_body(hidden, own, *refs):
    *others, out = refs
    x = hidden[...] + own[...]
    for o in others:
        x = x + o[...].astype(F32)
    out[...] = x.astype(BF16)


def bind(body, *first):
    def bound(*refs):
        return body(*first, *refs)

    return bound


def per_device(
    q_nope, q_rope, w_uk, w_uv, prompt, w_out, residual, routes, route_scores,
    expert_gate, expert_up, expert_down,
):
    rows, heads, nope = q_nope.shape
    lat, vdim = w_uk.shape[2], w_uv.shape[2]
    n_grp, n_ctx = lax.axis_size("grp"), lax.axis_size("ctx")
    count, width = residual.shape
    top = routes.shape[1]
    experts, _, ff = expert_gate.shape
    cap = CAP * n_ctx
    hid = ff // 2
    half = rows // 2
    hv = heads * vdim
    tail = -(-width // LANES) * LANES
    far = n_ctx // 2
    in_vmem = lambda a: pltpu.with_memory_space_constraint(a, VMEM)

    keys = prompt.T
    keep, send = run(
        "attend", attend_body, [((half, hv + LANES), F32), ((half, hv + LANES), BF16)],
        [q_nope, q_rope, w_uk, w_uv, keys],
        scratch=[
            VMEM(q_nope.shape, BF16), VMEM(q_rope.shape, BF16), VMEM(w_uk.shape, BF16),
            VMEM(w_uv.shape, BF16), VMEM(keys.shape, BF16), VMEM((rows, hv + LANES), F32),
            pltpu.SemaphoreType.DMA((3 + 2 * (heads // min(4, heads)),)),
        ],
        us=6, limit=16, hbm=range(5),
    )
    keep, send = run(
        "pair", bind(pair_body, heads), [((half, hv + LANES), F32), ((half, hv + LANES), BF16)],
        [keep, swap(send, "grp", 1)], us=3,
    )
    (mine,) = run(
        "merge", bind(final_body, heads), [((half, hv), BF16)], [keep] + spread(send, "grp"), us=5
    )
    keep, send, info = run(
        "project", project_body,
        [((rows // 2, width), F32), ((rows // 2, tail + LANES), BF16), ((count, LANES), F32)],
        [mine, swap(mine, "grp", 1), routes, route_scores, in_vmem(w_out)],
        scratch=[VMEM((rows, hv), BF16), VMEM((rows, width), F32), VMEM((16, LANES), F32)], us=3,
    )
    own, *sends, info = run(
        "rows", bind(pair_rows_body, True),
        [((count, width), F32)] + [((count, tail + LANES), BF16)] * (far - 1) + [((count, LANES), F32)],
        [keep, swap(send, "ctx", 1), info], us=5,
    )
    got = [swap(x, "ctx", 2 * s) for s, x in enumerate(sends, 1)]
    hidden, moe = run(
        "hidden", hidden_body, [((count, width), F32), ((count, width), BF16)],
        [own, residual] + got, us=5,
    )
    parts = spread(moe, "ctx")
    pick, mix = run(
        "route", bind(route_body, experts, top),
        [((experts * cap, rows), BF16), ((rows, experts * cap), F32)], [info] + got, us=1,
    )
    (near,) = run("gather", rows_body, [((rows // 2, width), BF16)], [moe] + parts, us=5)
    far_rows = swap(near, "ctx", 1)
    gate, up, down = in_vmem(expert_gate), in_vmem(expert_up), in_vmem(expert_down)
    size = max(1, experts // 2)
    groups = [range(i, i + size) for i in range(0, experts, size)]
    shape = (size, cap, 2 * hid)
    sent = []
    for g in groups:
        if not sent:
            x, send = run(
                "other_half", bind(first_half_body, g), [((experts * cap, width), BF16), (shape, BF16)],
                [pick, near, far_rows, gate, up], us=2,
            )
        else:
            (send,) = run(
                "other_half", bind(next_half_body, g), [(shape, BF16)], [x, gate, up], us=1.5
            )
        sent.append(swap(send, "grp", 1))
    sums = []
    for g, other in zip(groups, sent):
        keep, send = run(
            "own_half", bind(own_half_body, g), [(shape, F32), (shape, BF16)],
            [x, gate, up, other], us=1.5,
        )
        sums.append((keep, spread(send, "grp")))
    acts = []
    for keep, others in sums:
        (act,) = run("act", act_body, [((size, cap, hid), BF16)], [keep] + others, us=0.5)
        acts.append((act, swap(act, "grp", 1)))
    so_far = []
    for g, (act, other) in zip(groups, acts):
        last = g is groups[-1]
        outs = [((rows // 2, width), F32), ((rows // 2, width), BF16)] if last else [((rows, width), F32)]
        so_far = run(
            "down", bind(down_body, g, last), outs, [act, other, down, mix] + list(so_far), us=1.5
        )
    keep, send = so_far
    own, *sends = run(
        "rows2", bind(pair_rows_body, False),
        [((count, width), F32)] + [((count, width), BF16)] * (far - 1),
        [keep, swap(send, "ctx", 1)], us=3,
    )
    got = [swap(x, "ctx", 2 * s) for s, x in enumerate(sends, 1)]
    (out,) = run("out", out_body, [((count, width), BF16)], [hidden, own] + got, us=1)
    return out


def solution(mesh):
    in_specs = (
        P(None, "ctx", None),
        P(None, "ctx", None),
        P("ctx", None, None),
        P("ctx", None, None),
        P("grp", None),
        P("ctx", "grp"),
        P("ctx", "grp"),
        P("ctx", None),
        P("ctx", None),
        P("ctx", "grp", None),
        P("ctx", "grp", None),
        P("ctx", None, "grp"),
    )
    return jax.shard_map(
        per_device, mesh=mesh, in_specs=in_specs, out_specs=P("ctx", "grp"), check_vma=False
    )
```

```python
import jax
import jax.numpy as jnp
from jax import lax
from jax.experimental import pallas as pl
from jax.experimental.pallas import tpu as pltpu
from jax.sharding import PartitionSpec as P

CAP = 4
LANES = 128
route_factor = 2.5
F32 = jnp.float32
BF16 = jnp.bfloat16
VMEM = pltpu.VMEM


def swap(x, axis, bits):
    return lax.ppermute(x, axis, [(a, a ^ bits) for a in range(lax.axis_size(axis))])


def far_first(axis):
    return range(lax.axis_size(axis) // 2 - 1, 0, -1)


def spread(x, axis):
    return [swap(x, axis, 2 * s) for s in far_first(axis)]


def scatter(parts, axis):
    return [swap(parts[s - 1], axis, 2 * s) for s in far_first(axis)]


def run(name, body, outs, ins, scratch=(), us=1.0, limit=3, hbm=(), after=()):
    n_ins, n_after = len(ins), len(after)
    ins = [
        pltpu.with_memory_space_constraint(a, pltpu.HBM) if i in hbm else a
        for i, a in enumerate(ins)
    ]

    def ordered(*refs):
        return body(*refs[:n_ins], *refs[n_ins + n_after :])

    return pl.pallas_call(
        ordered,
        out_shape=[jax.ShapeDtypeStruct(s, d) for s, d in outs],
        in_specs=[
            pl.BlockSpec(memory_space=pltpu.HBM if i in hbm else VMEM) for i in range(n_ins)
        ]
        + [pl.BlockSpec(memory_space=pl.ANY)] * n_after,
        out_specs=[pl.BlockSpec(memory_space=VMEM) for _ in outs],
        scratch_shapes=list(scratch),
        cost_estimate=pl.CostEstimate(
            flops=int(us * 1.15e9), bytes_accessed=1024, transcendentals=0
        ),
        compiler_params=pltpu.CompilerParams(vmem_limit_bytes=limit << 20),
        name=name,
    )(*ins, *after)


def split3(x):
    hi = x.astype(BF16).astype(F32)
    mid = (x - hi).astype(BF16).astype(F32)
    return hi, mid, x - hi - mid


def pack_lse(x, heads):
    hi, mid, lo = split3(x)
    return (hi + pltpu.roll(mid, heads, 1) + pltpu.roll(lo, 2 * heads, 1)).astype(BF16)


def unpack_lse(x, heads):
    x = x.astype(F32)
    x = x + pltpu.roll(x, LANES - heads, 1) + pltpu.roll(x, LANES - 2 * heads, 1)
    lane = lax.broadcasted_iota(jnp.int32, x.shape, 1)
    return jnp.where(lane < heads, x, 0.0)


def attend_body(qn_h, qr_h, wuk_h, wuv_h, prompt_h, keep, send, qn, qr, wuk, wuv, prompt, rows_scr, sems):
    rows, heads, nope = qn.shape
    lat, vdim = wuk.shape[2], wuv.shape[2]
    half, width = rows // 2, heads * vdim
    group = min(4, heads)
    steps = heads // group
    core = lax.axis_index("grp") & 1
    copies = [
        pltpu.make_async_copy(qn_h, qn, sems.at[0]),
        pltpu.make_async_copy(qr_h, qr, sems.at[1]),
        pltpu.make_async_copy(prompt_h, prompt, sems.at[2]),
    ]
    uk = [
        pltpu.make_async_copy(
            wuk_h.at[pl.ds(c * group, group)], wuk.at[pl.ds(c * group, group)], sems.at[3 + c]
        )
        for c in range(steps)
    ]
    uv = [
        pltpu.make_async_copy(
            wuv_h.at[pl.ds(c * group, group)], wuv.at[pl.ds(c * group, group)], sems.at[3 + steps + c]
        )
        for c in range(steps)
    ]
    copies[0].start()
    uk[0].start()
    copies[1].start()
    copies[2].start()
    for c in range(steps):
        if c:
            uk[c].start()
        uv[c].start()
    scale = (nope + qr.shape[2]) ** (-0.5)
    copies[0].wait()
    queries = jnp.swapaxes(qn[...], 0, 1)
    copies[1].wait()
    turned = jnp.swapaxes(qr[...], 0, 1)
    lane = lax.broadcasted_iota(jnp.int32, (rows, LANES), 1)
    lse = jnp.zeros((rows, LANES), F32)
    for c in range(steps):
        own = range(c * group, (c + 1) * group)
        uk[c].wait()
        q = jnp.concatenate(
            [jnp.dot(queries[h], wuk[h], preferred_element_type=F32).astype(BF16) for h in own], 0
        )
        r = jnp.concatenate([turned[h] for h in own], 0)
        if c == 0:
            copies[2].wait()
        s = jnp.dot(q, prompt[:lat], preferred_element_type=F32)
        s = (s + jnp.dot(r, prompt[lat:], preferred_element_type=F32)) * scale
        top = jnp.max(s, -1, keepdims=True)
        p = jnp.exp(s - top)
        total = jnp.sum(p, -1, keepdims=True)
        w = lax.dot_general(
            p.astype(BF16), prompt[:lat], (((1,), (1,)), ((), ())), preferred_element_type=F32
        )
        w = w * (1.0 / total)
        hi = w.astype(BF16)
        lo = (w - hi.astype(F32)).astype(BF16)
        part = top + jnp.log(total)
        uv[c].wait()
        for i, h in enumerate(own):
            at = slice(i * rows, (i + 1) * rows)
            v = jnp.dot(jnp.concatenate([hi[at], lo[at]], 0), wuv[h], preferred_element_type=F32)
            rows_scr[:, h * vdim : (h + 1) * vdim] = v[:rows] + v[rows:]
            lse = jnp.where(lane == h, part[at], lse)
    rows_scr[:, width:] = lse
    keep[...] = rows_scr[pl.ds(pl.multiple_of(core * half, half), half)]
    out = rows_scr[pl.ds(pl.multiple_of((1 - core) * half, half), half)]
    send[:, :width] = out[:, :width].astype(BF16)
    send[:, width:] = pack_lse(out[:, width:], heads)


def merge_values(heads, own, others):
    width = own.shape[1] - LANES
    vdim = width // heads
    levels = [own[:, width:]] + [unpack_lse(o[:, width:], heads) for o in others]
    top = levels[0]
    for x in levels[1:]:
        top = jnp.maximum(top, x)
    raised = [jnp.exp(x - top) for x in levels]
    total = sum(raised)
    shares = [x / total for x in raised]
    cols = []
    for h in range(heads):
        at = slice(h * vdim, (h + 1) * vdim)
        v = own[:, at] * shares[0][:, h : h + 1]
        for share, o in zip(shares[1:], others):
            v = v + o[:, at].astype(F32) * share[:, h : h + 1]
        cols.append(v)
    lane = lax.broadcasted_iota(jnp.int32, top.shape, 1)
    return cols, jnp.where(lane < heads, top + jnp.log(total), 0.0)


def pair_body(heads, own, other, keep, send):
    width = own.shape[1] - LANES
    vdim = width // heads
    cols, lse = merge_values(heads, own, [other])
    for h, v in enumerate(cols):
        keep[:, h * vdim : (h + 1) * vdim] = v
        send[:, h * vdim : (h + 1) * vdim] = v.astype(BF16)
    keep[:, width:] = lse
    send[:, width:] = pack_lse(lse, heads)


def final_body(heads, own, *refs):
    out = refs[-1]
    vdim = (own.shape[1] - LANES) // heads
    cols, _ = merge_values(heads, own, refs[:-1])
    for h, v in enumerate(cols):
        out[:, h * vdim : (h + 1) * vdim] = v.astype(BF16)


def project_body(mine, other, routes, scores, w, keep, *refs):
    *sends, info, att, res, pad = refs
    half = mine.shape[0]
    width = w.shape[1]
    tail = sends[0].shape[1] - LANES
    count, top = routes.shape
    core = lax.axis_index("grp") & 1
    ctx = lax.axis_index("ctx")
    att[pl.ds(pl.multiple_of(core * half, half), half)] = mine[...]
    att[pl.ds(pl.multiple_of((1 - core) * half, half), half)] = other[...]
    res[...] = jnp.dot(att[...], w[...], preferred_element_type=F32)

    def block(turn, s):
        owner = ctx ^ (2 * s + turn)
        return res[pl.ds(pl.multiple_of(owner * count, count), count)]

    v = scores[...]
    v = route_factor * v / jnp.sum(v, -1, keepdims=True)
    hi, mid, lo = split3(v)
    pad[...] = jnp.zeros_like(pad)
    for i, x in enumerate((routes[...].astype(F32), hi, mid, lo)):
        pad[:count, i * top : (i + 1) * top] = x
    info[...] = pad[:count]
    wide = pad[...].astype(BF16)
    for s, send in enumerate(sends, 1):
        send[:, :width] = jnp.concatenate([block(0, s), block(1, s)], 0).astype(BF16)
        if tail > width:
            send[:, width:tail] = jnp.zeros((2 * count, tail - width), BF16)
        send[:, tail:] = wide
    keep[:count] = block(0, 0)
    keep[count:] = block(1, 0)


def rest_sum_body(distances, keep, residual, info, *refs):
    *others, own, send = refs
    count = residual.shape[0]
    width = own.shape[1]
    tail = others[0].shape[1] - LANES
    x = keep[...]
    for o in others:
        x = x + o[:, :width].astype(F32)
    own[:count] = x[:count] + residual[...].astype(F32)
    own[count:] = x[count:]
    send[:, :width] = own[...].astype(BF16)
    if tail > width:
        send[:, width:tail] = jnp.zeros((2 * count, tail - width), BF16)
    per = LANES // 32
    tables = {s: o[:, tail:].astype(F32) for s, o in zip(distances, others)}
    tables[0] = jnp.concatenate([info[...], jnp.zeros_like(info)], 0)
    for i in range((len(tables) + per - 1) // per):
        v = tables[i * per]
        for j in range(1, per):
            if i * per + j in tables:
                v = v + pltpu.roll(tables[i * per + j], 32 * j, 1)
        send[:, tail + i * LANES : tail + (i + 1) * LANES] = v.astype(BF16)


def hidden_body(own, other, hidden, moe):
    count, width = hidden.shape
    o = other[:, :width].astype(F32)
    x = own[...] + jnp.concatenate([o[count:], o[:count]], 0)
    hidden[...] = x[:count]
    moe[...] = x.astype(BF16)


def route_body(local_experts, top, width, mine, other, *refs):
    pick, mix = refs
    count = mine.shape[0] // 2
    far = lax.axis_size("ctx") // 2
    ctx = lax.axis_index("ctx")
    blocks = []
    per = LANES // 32
    for s in range(far):
        at = slice(width + s // per * LANES, width + (s // per + 1) * LANES)
        for ref in (mine, other):
            v = ref[:, at].astype(F32)[:count]
            blocks.append(pltpu.roll(v, (LANES - s % per * 32) % LANES, 1) if s % per else v)
    table = jnp.concatenate(blocks, 0)
    rows = table.shape[0]
    weights = (
        pltpu.roll(table, LANES - top, 1)
        + pltpu.roll(table, LANES - 2 * top, 1)
        + pltpu.roll(table, LANES - 3 * top, 1)
    )
    lane = lax.broadcasted_iota(jnp.int32, (rows, LANES), 1)
    hits, gains = [], []
    all_hits = jnp.zeros((rows, LANES), F32)
    for e in range(local_experts):
        named = (table == (ctx * local_experts + e).astype(F32)) & (lane < top)
        hit = jnp.sum(jnp.where(named, 1.0, 0.0), -1, keepdims=True)
        gains.append(jnp.sum(jnp.where(named, weights, 0.0), -1, keepdims=True))
        hits.append(hit)
        all_hits = jnp.where(lane == e, hit, all_hits)
    a = lax.broadcasted_iota(jnp.int32, (rows, rows), 0)
    b = lax.broadcasted_iota(jnp.int32, (rows, rows), 1)
    earlier = jnp.where((a // count == b // count) & (b < a), 1.0, 0.0).astype(BF16)
    rank = jnp.dot(earlier, all_hits.astype(BF16), preferred_element_type=F32)
    slots = mix.shape[1]
    cap = slots // local_experts
    wide = lax.broadcasted_iota(jnp.int32, (rows, slots), 1)
    start = lax.broadcasted_iota(jnp.int32, (rows, 1), 0) // count * CAP
    chosen = jnp.zeros((rows, slots), F32)
    gain = jnp.zeros((rows, slots), F32)
    for e in range(local_experts):
        slot = rank[:, e : e + 1].astype(jnp.int32) + start + e * cap
        at = (wide == slot) & (hits[e] > 0.5)
        chosen = jnp.where(at, 1.0, chosen)
        gain = jnp.where(at, gains[e], gain)
    pick[...] = jnp.transpose(chosen).astype(BF16)
    mix[...] = gain


def half_cols(hid, mine):
    core = lax.axis_index("grp") & 1
    return pl.ds(pl.multiple_of((core if mine else 1 - core) * hid, hid), hid)


def half_products(experts, mine, x, gate, up, out):
    hid = out.shape[2] // 2
    cap = out.shape[1]
    cols = half_cols(hid, mine)
    for i, e in enumerate(experts):
        xe = x[e * cap : (e + 1) * cap]
        for j, w in enumerate((gate, up)):
            v = jnp.dot(xe, w[e, :, cols], preferred_element_type=F32)
            out[i, :, j * hid : (j + 1) * hid] = v.astype(out.dtype)


def first_half_body(experts, pick, gate, up, *refs):
    *parts, x, send = refs
    rows = jnp.concatenate([p[...] for p in parts], 0)
    x[...] = jnp.dot(pick[...], rows, preferred_element_type=F32).astype(BF16)
    half_products(experts, False, x, gate, up, send)


def half_body(experts, mine, x, gate, up, out):
    half_products(experts, mine, x, gate, up, out)


def add_body(experts, x, other, keep, send):
    for i, e in enumerate(experts):
        v = x[i] + other[e].astype(F32)
        keep[i] = v
        send[i] = v.astype(BF16)


def act_body(keep, *refs):
    *others, out = refs
    hid = out.shape[2]
    for i in range(out.shape[0]):
        x = keep[i]
        for o in others:
            x = x + o[i].astype(F32)
        gate, up = x[:, :hid], x[:, hid:]
        out[i] = (gate / (1.0 + jnp.exp(-gate)) * up).astype(BF16)


def weigh(experts, cap, mix, parts):
    result = jnp.concatenate([v.astype(BF16) for v in parts], 0)
    gain = mix[:, experts[0] * cap : (experts[-1] + 1) * cap]
    hi = gain.astype(BF16)
    lo = (gain - hi.astype(F32)).astype(BF16)
    v = jnp.dot(hi, result, preferred_element_type=F32)
    return v + jnp.dot(lo, result, preferred_element_type=F32)


def down_body(experts, mine, other, down, mix, out):
    hid = mine.shape[2]
    low, high = half_cols(hid, True), half_cols(hid, False)
    parts = []
    for i, e in enumerate(experts):
        v = jnp.dot(mine[i], down[e, low], preferred_element_type=F32)
        parts.append(v + jnp.dot(other[i], down[e, high], preferred_element_type=F32))
    out[...] = weigh(experts, mine.shape[1], mix, parts)


def down_mine_body(experts, mine, down, out):
    low = half_cols(mine.shape[2], True)
    for i, e in enumerate(experts):
        out[i] = jnp.dot(mine[i], down[e, low], preferred_element_type=F32)


def down_last_body(has_before, experts, part, other, down, mix, *refs):
    high = half_cols(other.shape[2], False)
    parts = [
        part[i] + jnp.dot(other[i], down[e, high], preferred_element_type=F32)
        for i, e in enumerate(experts)
    ]
    v = weigh(experts, other.shape[1], mix, parts)
    if has_before:
        v = v + refs[0][...]
        refs = refs[1:]
    keep, *sends = refs
    n = keep.shape[0]
    keep[...] = v[:n]
    for s, send in enumerate(sends, 1):
        send[...] = v[s * n : (s + 1) * n].astype(BF16)


def last_sum_body(keep, *refs):
    *others, own, send = refs
    count = own.shape[0]
    x = keep[...]
    for o in others:
        x = x + o[...].astype(F32)
    own[...] = x[:count]
    send[...] = x[count:].astype(BF16)


def out_body(hidden, own, other, out):
    out[...] = (hidden[...] + own[...] + other[...].astype(F32)).astype(BF16)


def bind(body, *first):
    def bound(*refs):
        return body(*first, *refs)

    return bound


def per_device(
    q_nope, q_rope, w_uk, w_uv, prompt, w_out, residual, routes, route_scores,
    expert_gate, expert_up, expert_down,
):
    rows, heads, nope = q_nope.shape
    lat, vdim = w_uk.shape[2], w_uv.shape[2]
    n_grp, n_ctx = lax.axis_size("grp"), lax.axis_size("ctx")
    count, width = residual.shape
    top = routes.shape[1]
    experts, _, ff = expert_gate.shape
    cap = CAP * n_ctx
    hid = ff // 2
    half = rows // 2
    hv = heads * vdim
    tail = -(-width // LANES) * LANES
    far = n_ctx // 2
    in_vmem = lambda a: pltpu.with_memory_space_constraint(a, VMEM)

    keys = prompt.T
    keep, send = run(
        "attend", attend_body, [((half, hv + LANES), F32), ((half, hv + LANES), BF16)],
        [q_nope, q_rope, w_uk, w_uv, keys],
        scratch=[
            VMEM(q_nope.shape, BF16), VMEM(q_rope.shape, BF16), VMEM(w_uk.shape, BF16),
            VMEM(w_uv.shape, BF16), VMEM(keys.shape, BF16), VMEM((rows, hv + LANES), F32),
            pltpu.SemaphoreType.DMA((3 + 2 * (heads // min(4, heads)),)),
        ],
        us=12, limit=10, hbm=range(5),
    )
    keep, send = run(
        "pair", bind(pair_body, heads), [((half, hv + LANES), F32), ((half, hv + LANES), BF16)],
        [keep, swap(send, "grp", 1)], us=1,
    )
    (mine,) = run(
        "merge", bind(final_body, heads), [((half, hv), BF16)], [keep] + spread(send, "grp"), us=1
    )
    pair = 2 * count
    keep, *sends, info = run(
        "project", project_body,
        [((pair, width), F32)] + [((pair, tail + LANES), BF16)] * (far - 1) + [((count, LANES), F32)],
        [mine, swap(mine, "grp", 1), routes, route_scores, in_vmem(w_out)],
        scratch=[VMEM((rows, hv), BF16), VMEM((rows, width), F32), VMEM((pair, LANES), F32)], us=1,
    )
    wide = -(-32 * far // LANES) * LANES
    own, send = run(
        "rest_sum", bind(rest_sum_body, list(far_first("ctx"))),
        [((pair, width), F32), ((pair, tail + wide), BF16)],
        [keep, residual, info] + scatter(sends, "ctx"), us=1,
    )
    other = swap(send, "ctx", 1)
    hidden, moe = run(
        "hidden", hidden_body, [((count, width), F32), ((pair, width), BF16)], [own, other], us=1
    )
    parts = dict(zip(far_first("ctx"), spread(moe, "ctx")))
    parts[0] = moe
    pick, mix = run(
        "route", bind(route_body, experts, top, tail),
        [((experts * cap, rows), BF16), ((rows, experts * cap), F32)], [send, other], us=0.5,
    )
    gate, up, down = in_vmem(expert_gate), in_vmem(expert_up), in_vmem(expert_down)
    size = max(1, experts // 2)
    groups = [range(i, i + size) for i in range(0, experts, size)]
    shape = (size, cap, 2 * hid)
    whole = (experts, cap, 2 * hid)
    x, send = run(
        "other_half", bind(first_half_body, range(experts)),
        [((experts * cap, width), BF16), (whole, BF16)],
        [pick, gate, up] + [parts[s] for s in range(far)], us=0.5,
    )
    other = swap(send, "grp", 1)
    sums = []
    for g in groups:
        (part,) = run(
            "own_half", bind(half_body, g, True), [(shape, F32)], [x, gate, up], us=0.5 if sums else 0.5,
            after=[sums[-1][0] if sums else send],
        )
        keep, send = run(
            "add", bind(add_body, g), [(shape, F32), (shape, BF16)], [part, other], us=0.1
        )
        sums.append((keep, spread(send, "grp")))
    before = []
    for g, (keep, others) in zip(groups, sums):
        (act,) = run(
            "act", act_body, [((size, cap, hid), BF16)], [keep] + others, us=5, after=before if before else [sums[-1][0]]
        )
        other = swap(act, "grp", 1)
        if g is not groups[-1]:
            before = list(run(
                "down", bind(down_body, g), [((rows, width), F32)], [act, other, down, mix], us=0.5
            ))
        else:
            (part,) = run(
                "down_mine", bind(down_mine_body, g), [((size, cap, width), F32)], [act, down], us=0.5
            )
            keep, *sends = run(
                "down_last", bind(down_last_body, len(before), g),
                [((pair, width), F32)] + [((pair, width), BF16)] * (far - 1),
                [part, other, down, mix] + before, us=5,
            )
    own, send = run(
        "last_sum", last_sum_body, [((count, width), F32), ((count, width), BF16)],
        [keep] + scatter(sends, "ctx"), us=3,
    )
    (out,) = run(
        "out", out_body, [((count, width), BF16)], [hidden, own, swap(send, "ctx", 1)], us=1
    )
    return out


def solution(mesh):
    in_specs = (
        P(None, "ctx", None),
        P(None, "ctx", None),
        P("ctx", None, None),
        P("ctx", None, None),
        P("grp", None),
        P("ctx", "grp"),
        P("ctx", "grp"),
        P("ctx", None),
        P("ctx", None),
        P("ctx", "grp", None),
        P("ctx", "grp", None),
        P("ctx", None, "grp"),
    )
    return jax.shard_map(
        per_device, mesh=mesh, in_specs=in_specs, out_specs=P("ctx", "grp"), check_vma=False
    )
```

```python
import jax
import jax.numpy as jnp
from jax import lax
from jax.experimental import pallas as pl
from jax.experimental.pallas import tpu as pltpu
from jax.sharding import PartitionSpec as P

CAP = 4
LANES = 128
route_factor = 2.5
F32 = jnp.float32
BF16 = jnp.bfloat16
VMEM = pltpu.VMEM


def swap(x, axis, bits):
    return lax.ppermute(x, axis, [(a, a ^ bits) for a in range(lax.axis_size(axis))])


def far_first(axis):
    return range(lax.axis_size(axis) // 2 - 1, 0, -1)


def spread(x, axis):
    return [swap(x, axis, 2 * s) for s in far_first(axis)]


def scatter(parts, axis):
    return [swap(parts[s - 1], axis, 2 * s) for s in far_first(axis)]


def run(name, body, outs, ins, scratch=(), us=1.0, limit=3, hbm=(), after=()):
    n_ins, n_after = len(ins), len(after)
    ins = [
        pltpu.with_memory_space_constraint(a, pltpu.HBM) if i in hbm else a
        for i, a in enumerate(ins)
    ]

    def ordered(*refs):
        return body(*refs[:n_ins], *refs[n_ins + n_after :])

    return pl.pallas_call(
        ordered,
        out_shape=[jax.ShapeDtypeStruct(s, d) for s, d in outs],
        in_specs=[
            pl.BlockSpec(memory_space=pltpu.HBM if i in hbm else VMEM) for i in range(n_ins)
        ]
        + [pl.BlockSpec(memory_space=pl.ANY)] * n_after,
        out_specs=[pl.BlockSpec(memory_space=VMEM) for _ in outs],
        scratch_shapes=list(scratch),
        cost_estimate=pl.CostEstimate(
            flops=int(us * 1.15e9), bytes_accessed=1024, transcendentals=0
        ),
        compiler_params=pltpu.CompilerParams(vmem_limit_bytes=limit << 20),
        name=name,
    )(*ins, *after)


def split3(x):
    hi = x.astype(BF16).astype(F32)
    mid = (x - hi).astype(BF16).astype(F32)
    return hi, mid, x - hi - mid


def pack_lse(x, heads):
    hi, mid, lo = split3(x)
    return (hi + pltpu.roll(mid, heads, 1) + pltpu.roll(lo, 2 * heads, 1)).astype(BF16)


def unpack_lse(x, heads):
    x = x.astype(F32)
    x = x + pltpu.roll(x, LANES - heads, 1) + pltpu.roll(x, LANES - 2 * heads, 1)
    lane = lax.broadcasted_iota(jnp.int32, x.shape, 1)
    return jnp.where(lane < heads, x, 0.0)


def query_body(qn_h, qr_h, wuk_h, keys_h, queries, turned, keys, qn, qr, wuk, nope_scr, rope_scr, sems):
    rows, heads, _ = qn.shape
    half = heads // 2
    group = min(4, half)
    steps = half // group
    first = (lax.axis_index("grp") & 1) * half
    copies = [
        pltpu.make_async_copy(qn_h, qn, sems.at[0]),
        pltpu.make_async_copy(qr_h, qr, sems.at[1]),
        pltpu.make_async_copy(keys_h, keys, sems.at[2]),
    ]
    uk = [
        pltpu.make_async_copy(
            wuk_h.at[pl.ds(first + c * group, group)], wuk.at[pl.ds(c * group, group)], sems.at[3 + c]
        )
        for c in range(steps)
    ]
    for copy in [copies[0], uk[0], copies[1]] + uk[1:] + [copies[2]]:
        copy.start()
    copies[0].wait()
    nope_scr[...] = jnp.swapaxes(qn[...], 0, 1)
    copies[1].wait()
    rope_scr[...] = jnp.swapaxes(qr[...], 0, 1)
    for h in range(half):
        turned[h * rows : (h + 1) * rows] = rope_scr[first + h]
        if h % group == 0:
            uk[h // group].wait()
        q = jnp.dot(nope_scr[first + h], wuk[h], preferred_element_type=F32)
        queries[h * rows : (h + 1) * rows] = q.astype(BF16)
    copies[2].wait()


def attend_body(scale, queries, turned, mine, other, wuv_h, keep, send, wuv, sems):
    heads, lat, vdim = wuv.shape
    rows = keep.shape[0]
    width = heads * vdim
    first = (lax.axis_index("grp") & 1) * heads
    copy = pltpu.make_async_copy(wuv_h.at[pl.ds(first, heads)], wuv, sems.at[0])
    copy.start()
    q, r = queries[...], turned[...]
    keys = (mine, other)
    scores = []
    for k in keys:
        s = jnp.dot(q, k[:lat], preferred_element_type=F32)
        scores.append((s + jnp.dot(r, k[lat:], preferred_element_type=F32)) * scale)
    top = jnp.max(jnp.maximum(*scores), -1, keepdims=True)
    total, w = 0.0, 0.0
    for s, k in zip(scores, keys):
        p = jnp.exp(s - top)
        total = total + jnp.sum(p, -1, keepdims=True)
        w = w + lax.dot_general(
            p.astype(BF16), k[:lat], (((1,), (1,)), ((), ())), preferred_element_type=F32
        )
    w = w * (1.0 / total)
    hi = w.astype(BF16)
    lo = (w - hi.astype(F32)).astype(BF16)
    level = top + jnp.log(total)
    lane = lax.broadcasted_iota(jnp.int32, (rows, LANES), 1)
    lse = jnp.zeros((rows, LANES), F32)
    copy.wait()
    for h in range(heads):
        at = slice(h * rows, (h + 1) * rows)
        v = jnp.dot(jnp.concatenate([hi[at], lo[at]], 0), wuv[h], preferred_element_type=F32)
        v = v[:rows] + v[rows:]
        keep[:, h * vdim : (h + 1) * vdim] = v
        send[:, h * vdim : (h + 1) * vdim] = v.astype(BF16)
        lse = jnp.where(lane == h, level[at], lse)
    keep[:, width:] = lse
    send[:, width:] = pack_lse(lse, heads)


def merge_body(heads, own, *refs):
    *others, out = refs
    width = out.shape[1]
    vdim = width // heads
    levels = [own[:, width:]] + [unpack_lse(o[:, width:], heads) for o in others]
    top = levels[0]
    for x in levels[1:]:
        top = jnp.maximum(top, x)
    raised = [jnp.exp(x - top) for x in levels]
    total = sum(raised)
    shares = [x / total for x in raised]
    for h in range(heads):
        at = slice(h * vdim, (h + 1) * vdim)
        v = own[:, at] * shares[0][:, h : h + 1]
        for share, o in zip(shares[1:], others):
            v = v + o[:, at].astype(F32) * share[:, h : h + 1]
        out[:, at] = v.astype(BF16)


def head_rows(width, mine):
    core = lax.axis_index("grp") & 1
    return pl.ds(pl.multiple_of((core if mine else 1 - core) * width, width), width)


def project_mine_body(mine, w, out):
    out[...] = jnp.dot(mine[...], w[head_rows(mine.shape[1], True)], preferred_element_type=F32)


def project_body(part, other, routes, scores, w, keep, *refs):
    *sends, info, res, pad = refs
    width = w.shape[1]
    tail = sends[0].shape[1] - LANES
    count, top = routes.shape
    ctx = lax.axis_index("ctx")
    res[...] = part[...] + jnp.dot(
        other[...], w[head_rows(other.shape[1], False)], preferred_element_type=F32
    )

    def block(turn, s):
        owner = ctx ^ (2 * s + turn)
        return res[pl.ds(pl.multiple_of(owner * count, count), count)]

    v = scores[...]
    v = route_factor * v / jnp.sum(v, -1, keepdims=True)
    hi, mid, lo = split3(v)
    pad[...] = jnp.zeros_like(pad)
    for i, x in enumerate((routes[...].astype(F32), hi, mid, lo)):
        pad[:count, i * top : (i + 1) * top] = x
    info[...] = pad[:count]
    wide = pad[...].astype(BF16)
    for s, send in enumerate(sends, 1):
        send[:, :width] = jnp.concatenate([block(0, s), block(1, s)], 0).astype(BF16)
        if tail > width:
            send[:, width:tail] = jnp.zeros((2 * count, tail - width), BF16)
        send[:, tail:] = wide
    keep[:count] = block(0, 0)
    keep[count:] = block(1, 0)


def rest_sum_body(distances, keep, residual, info, *refs):
    *others, own, send = refs
    count = residual.shape[0]
    width = own.shape[1]
    tail = others[0].shape[1] - LANES
    x = keep[...]
    for o in others:
        x = x + o[:, :width].astype(F32)
    own[:count] = x[:count] + residual[...].astype(F32)
    own[count:] = x[count:]
    send[:, :width] = own[...].astype(BF16)
    if tail > width:
        send[:, width:tail] = jnp.zeros((2 * count, tail - width), BF16)
    per = LANES // 32
    tables = {s: o[:, tail:].astype(F32) for s, o in zip(distances, others)}
    tables[0] = jnp.concatenate([info[...], jnp.zeros_like(info)], 0)
    for i in range((len(tables) + per - 1) // per):
        v = tables[i * per]
        for j in range(1, per):
            if i * per + j in tables:
                v = v + pltpu.roll(tables[i * per + j], 32 * j, 1)
        send[:, tail + i * LANES : tail + (i + 1) * LANES] = v.astype(BF16)


def hidden_body(own, other, hidden, moe):
    count, width = hidden.shape
    o = other[:, :width].astype(F32)
    x = own[...] + jnp.concatenate([o[count:], o[:count]], 0)
    hidden[...] = x[:count]
    moe[...] = x.astype(BF16)


def route_body(local_experts, top, width, mine, other, *refs):
    pick, mix = refs
    count = mine.shape[0] // 2
    far = lax.axis_size("ctx") // 2
    ctx = lax.axis_index("ctx")
    blocks = []
    per = LANES // 32
    for s in range(far):
        at = slice(width + s // per * LANES, width + (s // per + 1) * LANES)
        for ref in (mine, other):
            v = ref[:, at].astype(F32)[:count]
            blocks.append(pltpu.roll(v, (LANES - s % per * 32) % LANES, 1) if s % per else v)
    table = jnp.concatenate(blocks, 0)
    rows = table.shape[0]
    weights = (
        pltpu.roll(table, LANES - top, 1)
        + pltpu.roll(table, LANES - 2 * top, 1)
        + pltpu.roll(table, LANES - 3 * top, 1)
    )
    lane = lax.broadcasted_iota(jnp.int32, (rows, LANES), 1)
    hits, gains = [], []
    all_hits = jnp.zeros((rows, LANES), F32)
    for e in range(local_experts):
        named = (table == (ctx * local_experts + e).astype(F32)) & (lane < top)
        hit = jnp.sum(jnp.where(named, 1.0, 0.0), -1, keepdims=True)
        gains.append(jnp.sum(jnp.where(named, weights, 0.0), -1, keepdims=True))
        hits.append(hit)
        all_hits = jnp.where(lane == e, hit, all_hits)
    a = lax.broadcasted_iota(jnp.int32, (rows, rows), 0)
    b = lax.broadcasted_iota(jnp.int32, (rows, rows), 1)
    earlier = jnp.where((a // count == b // count) & (b < a), 1.0, 0.0).astype(BF16)
    rank = jnp.dot(earlier, all_hits.astype(BF16), preferred_element_type=F32)
    slots = mix.shape[1]
    cap = slots // local_experts
    wide = lax.broadcasted_iota(jnp.int32, (rows, slots), 1)
    start = lax.broadcasted_iota(jnp.int32, (rows, 1), 0) // count * CAP
    chosen = jnp.zeros((rows, slots), F32)
    gain = jnp.zeros((rows, slots), F32)
    for e in range(local_experts):
        slot = rank[:, e : e + 1].astype(jnp.int32) + start + e * cap
        at = (wide == slot) & (hits[e] > 0.5)
        chosen = jnp.where(at, 1.0, chosen)
        gain = jnp.where(at, gains[e], gain)
    pick[...] = jnp.transpose(chosen).astype(BF16)
    mix[...] = gain


def half_cols(hid, mine):
    core = lax.axis_index("grp") & 1
    return pl.ds(pl.multiple_of((core if mine else 1 - core) * hid, hid), hid)


def half_products(experts, mine, x, gate, up, out):
    hid = out.shape[2] // 2
    cap = out.shape[1]
    cols = half_cols(hid, mine)
    for i, e in enumerate(experts):
        xe = x[e * cap : (e + 1) * cap]
        for j, w in enumerate((gate, up)):
            v = jnp.dot(xe, w[e, :, cols], preferred_element_type=F32)
            out[i, :, j * hid : (j + 1) * hid] = v.astype(out.dtype)


def first_half_body(experts, pick, gate, up, *refs):
    *parts, x, send = refs
    rows = jnp.concatenate([p[...] for p in parts], 0)
    x[...] = jnp.dot(pick[...], rows, preferred_element_type=F32).astype(BF16)
    half_products(experts, False, x, gate, up, send)


def half_body(experts, mine, x, gate, up, out):
    half_products(experts, mine, x, gate, up, out)


def add_body(experts, x, other, keep, send):
    for i, e in enumerate(experts):
        v = x[i] + other[e].astype(F32)
        keep[i] = v
        send[i] = v.astype(BF16)


def act_body(keep, *refs):
    *others, out = refs
    hid = out.shape[2]
    for i in range(out.shape[0]):
        x = keep[i]
        for o in others:
            x = x + o[i].astype(F32)
        gate, up = x[:, :hid], x[:, hid:]
        out[i] = (gate / (1.0 + jnp.exp(-gate)) * up).astype(BF16)


def weigh(experts, cap, mix, parts):
    result = jnp.concatenate([v.astype(BF16) for v in parts], 0)
    gain = mix[:, experts[0] * cap : (experts[-1] + 1) * cap]
    hi = gain.astype(BF16)
    lo = (gain - hi.astype(F32)).astype(BF16)
    v = jnp.dot(hi, result, preferred_element_type=F32)
    return v + jnp.dot(lo, result, preferred_element_type=F32)


def down_mine_body(experts, mine, down, out):
    low = half_cols(mine.shape[2], True)
    for i, e in enumerate(experts):
        out[i] = jnp.dot(mine[i], down[e, low], preferred_element_type=F32)


def down_next_body(experts, later, part, other, mine, down, mix, out, ahead):
    low, high = half_cols(mine.shape[2], True), half_cols(mine.shape[2], False)
    parts = [
        part[i] + jnp.dot(other[i], down[e, high], preferred_element_type=F32)
        for i, e in enumerate(experts)
    ]
    for i, e in enumerate(later):
        ahead[i] = jnp.dot(mine[i], down[e, low], preferred_element_type=F32)
    out[...] = weigh(experts, other.shape[1], mix, parts)


def down_last_body(has_before, experts, part, other, down, mix, *refs):
    high = half_cols(other.shape[2], False)
    parts = [
        part[i] + jnp.dot(other[i], down[e, high], preferred_element_type=F32)
        for i, e in enumerate(experts)
    ]
    v = weigh(experts, other.shape[1], mix, parts)
    if has_before:
        v = v + refs[0][...]
        refs = refs[1:]
    keep, *sends = refs
    n = keep.shape[0]
    keep[...] = v[:n]
    for s, send in enumerate(sends, 1):
        send[...] = v[s * n : (s + 1) * n].astype(BF16)


def last_sum_body(keep, *refs):
    *others, own, send = refs
    count = own.shape[0]
    x = keep[...]
    for o in others:
        x = x + o[...].astype(F32)
    own[...] = x[:count]
    send[...] = x[count:].astype(BF16)


def out_body(hidden, own, other, out):
    out[...] = (hidden[...] + own[...] + other[...].astype(F32)).astype(BF16)


def bind(body, *first):
    def bound(*refs):
        return body(*first, *refs)

    return bound


def per_device(
    q_nope, q_rope, w_uk, w_uv, prompt, w_out, residual, routes, route_scores,
    expert_gate, expert_up, expert_down,
):
    rows, heads, nope = q_nope.shape
    lat, vdim = w_uk.shape[2], w_uv.shape[2]
    n_grp, n_ctx = lax.axis_size("grp"), lax.axis_size("ctx")
    count, width = residual.shape
    top = routes.shape[1]
    experts, _, ff = expert_gate.shape
    cap = CAP * n_ctx
    hid = ff // 2
    hv = heads // 2 * vdim
    tail = -(-width // LANES) * LANES
    far = n_ctx // 2
    in_vmem = lambda a: pltpu.with_memory_space_constraint(a, VMEM)

    keys = prompt.T
    far_keys = swap(keys, "grp", 1)
    many = heads // 2 * rows
    queries, turned, keys = run(
        "queries", query_body,
        [((many, lat), BF16), ((many, q_rope.shape[2]), BF16), (keys.shape, BF16)],
        [q_nope, q_rope, w_uk, keys],
        scratch=[
            VMEM(q_nope.shape, BF16), VMEM(q_rope.shape, BF16), VMEM((heads // 2,) + w_uk.shape[1:], BF16),
            VMEM((heads, rows, nope), BF16), VMEM((heads, rows, q_rope.shape[2]), BF16),
            pltpu.SemaphoreType.DMA((3 + max(1, heads // 8),)),
        ],
        us=2, limit=6, hbm=range(4),
    )
    scale = (nope + q_rope.shape[2]) ** (-0.5)
    keep, send = run(
        "attend", bind(attend_body, scale), [((rows, hv + LANES), F32), ((rows, hv + LANES), BF16)],
        [queries, turned, keys, far_keys, w_uv],
        scratch=[VMEM((heads // 2,) + w_uv.shape[1:], BF16), pltpu.SemaphoreType.DMA((1,))],
        us=12, limit=12, hbm=(4,),
    )
    (mine,) = run(
        "merge", bind(merge_body, heads // 2), [((rows, hv), BF16)], [keep] + spread(send, "grp"), us=1
    )
    other = swap(mine, "grp", 1)
    w_out = in_vmem(w_out)
    (part,) = run("project_mine", project_mine_body, [((rows, width), F32)], [mine, w_out], us=0.5)
    pair = 2 * count
    keep, *sends, info = run(
        "project", project_body,
        [((pair, width), F32)] + [((pair, tail + LANES), BF16)] * (far - 1) + [((count, LANES), F32)],
        [part, other, routes, route_scores, w_out],
        scratch=[VMEM((rows, width), F32), VMEM((pair, LANES), F32)], us=1,
    )
    wide = -(-32 * far // LANES) * LANES
    own, send = run(
        "rest_sum", bind(rest_sum_body, list(far_first("ctx"))),
        [((pair, width), F32), ((pair, tail + wide), BF16)],
        [keep, residual, info] + scatter(sends, "ctx"), us=1,
    )
    other = swap(send, "ctx", 1)
    hidden, moe = run(
        "hidden", hidden_body, [((count, width), F32), ((pair, width), BF16)], [own, other], us=1
    )
    parts = dict(zip(far_first("ctx"), spread(moe, "ctx")))
    parts[0] = moe
    pick, mix = run(
        "route", bind(route_body, experts, top, tail),
        [((experts * cap, rows), BF16), ((rows, experts * cap), F32)], [send, other], us=0.5, after=[parts[far - 1]],
    )
    gate, up, down = in_vmem(expert_gate), in_vmem(expert_up), in_vmem(expert_down)
    size = -(-experts // 2)
    groups = [range(i, i + size) for i in range(0, experts, size)]
    shape = (size, cap, 2 * hid)
    whole = (experts, cap, 2 * hid)
    x, send = run(
        "other_half", bind(first_half_body, range(experts)),
        [((experts * cap, width), BF16), (whole, BF16)],
        [pick, gate, up] + [parts[s] for s in range(far)], us=0.5,
    )
    other = swap(send, "grp", 1)
    sums = []
    for g in groups:
        (part,) = run(
            "own_half", bind(half_body, g, True), [(shape, F32)], [x, gate, up], us=0.5 if sums else 0.5,
            after=[sums[-1][0] if sums else send],
        )
        keep, send = run(
            "add", bind(add_body, g), [(shape, F32), (shape, BF16)], [part, other], us=0.1
        )
        sums.append((keep, spread(send, "grp")))
    before, later = [], []
    for g, (keep, others) in zip(groups, sums):
        (act,) = run(
            "act", act_body, [((size, cap, hid), BF16)], [keep] + others, us=5,
            after=later or [sums[-1][0]],
        )
        other_act = swap(act, "grp", 1)
        if later:
            before, part = run(
                "down_next", bind(down_next_body, groups[0], g),
                [((rows, width), F32), ((size, cap, width), F32)],
                [later[0], last_act, act, down, mix], us=1,
            )
            before = [before]
        else:
            (part,) = run(
                "down_mine", bind(down_mine_body, g), [((size, cap, width), F32)], [act, down], us=0.5
            )
            later, last_act = [part], other_act
    keep, *sends = run(
        "down_last", bind(down_last_body, len(before), groups[-1]),
        [((pair, width), F32)] + [((pair, width), BF16)] * (far - 1),
        [part, other_act, down, mix] + before, us=1,
    )
    own, send = run(
        "last_sum", last_sum_body, [((count, width), F32), ((count, width), BF16)],
        [keep] + scatter(sends, "ctx"), us=3,
    )
    (out,) = run(
        "out", out_body, [((count, width), BF16)], [hidden, own, swap(send, "ctx", 1)], us=1
    )
    return out


def solution(mesh):
    in_specs = (
        P(None, "ctx", None),
        P(None, "ctx", None),
        P("ctx", None, None),
        P("ctx", None, None),
        P("grp", None),
        P("ctx", "grp"),
        P("ctx", "grp"),
        P("ctx", None),
        P("ctx", None),
        P("ctx", "grp", None),
        P("ctx", "grp", None),
        P("ctx", None, "grp"),
    )
    return jax.shard_map(
        per_device, mesh=mesh, in_specs=in_specs, out_specs=P("ctx", "grp"), check_vma=False
    )
```

```python
import jax
import jax.numpy as jnp
from jax import lax
from jax.experimental import pallas as pl
from jax.experimental.pallas import tpu as pltpu
from jax.sharding import PartitionSpec as P

CAP = 4
LANES = 128
route_factor = 2.5
F32 = jnp.float32
BF16 = jnp.bfloat16
VMEM = pltpu.VMEM


def swap(x, axis, bits):
    return lax.ppermute(x, axis, [(a, a ^ bits) for a in range(lax.axis_size(axis))])


def far_first(axis):
    return range(lax.axis_size(axis) // 2 - 1, 0, -1)


def spread(x, axis):
    return [swap(x, axis, 2 * s) for s in far_first(axis)]


def scatter(parts, axis):
    return [swap(parts[s - 1], axis, 2 * s) for s in far_first(axis)]


def run(name, body, outs, ins, scratch=(), us=1.0, limit=3, hbm=(), after=()):
    n_ins, n_after = len(ins), len(after)
    ins = [
        pltpu.with_memory_space_constraint(a, pltpu.HBM) if i in hbm else a
        for i, a in enumerate(ins)
    ]

    def ordered(*refs):
        return body(*refs[:n_ins], *refs[n_ins + n_after :])

    return pl.pallas_call(
        ordered,
        out_shape=[jax.ShapeDtypeStruct(s, d) for s, d in outs],
        in_specs=[
            pl.BlockSpec(memory_space=pltpu.HBM if i in hbm else VMEM) for i in range(n_ins)
        ]
        + [pl.BlockSpec(memory_space=pl.ANY)] * n_after,
        out_specs=[pl.BlockSpec(memory_space=VMEM) for _ in outs],
        scratch_shapes=list(scratch),
        cost_estimate=pl.CostEstimate(
            flops=int(us * 1.15e9), bytes_accessed=1024, transcendentals=0
        ),
        compiler_params=pltpu.CompilerParams(vmem_limit_bytes=limit << 20),
        name=name,
    )(*ins, *after)


def split3(x):
    hi = x.astype(BF16).astype(F32)
    mid = (x - hi).astype(BF16).astype(F32)
    return hi, mid, x - hi - mid


def pack_lse(x, heads):
    hi, mid, lo = split3(x)
    return (hi + pltpu.roll(mid, heads, 1) + pltpu.roll(lo, 2 * heads, 1)).astype(BF16)


def unpack_lse(x, heads):
    x = x.astype(F32)
    x = x + pltpu.roll(x, LANES - heads, 1) + pltpu.roll(x, LANES - 2 * heads, 1)
    lane = lax.broadcasted_iota(jnp.int32, x.shape, 1)
    return jnp.where(lane < heads, x, 0.0)


def query_body(qn_h, qr_h, wuk_h, keys_h, queries, turned, keys, qn, qr, wuk, nope_scr, rope_scr, sems):
    rows, heads, _ = qn.shape
    half = heads // 2
    group = min(4, half)
    steps = half // group
    first = (lax.axis_index("grp") & 1) * half
    copies = [
        pltpu.make_async_copy(qn_h, qn, sems.at[0]),
        pltpu.make_async_copy(qr_h, qr, sems.at[1]),
        pltpu.make_async_copy(keys_h, keys, sems.at[2]),
    ]
    uk = [
        pltpu.make_async_copy(
            wuk_h.at[pl.ds(first + c * group, group)], wuk.at[pl.ds(c * group, group)], sems.at[3 + c]
        )
        for c in range(steps)
    ]
    for copy in [copies[0], uk[0], copies[1]] + uk[1:] + [copies[2]]:
        copy.start()
    copies[0].wait()
    nope_scr[...] = jnp.swapaxes(qn[...], 0, 1)
    copies[1].wait()
    rope_scr[...] = jnp.swapaxes(qr[...], 0, 1)
    for h in range(half):
        turned[h * rows : (h + 1) * rows] = rope_scr[first + h]
        if h % group == 0:
            uk[h // group].wait()
        q = jnp.dot(nope_scr[first + h], wuk[h], preferred_element_type=F32)
        queries[h * rows : (h + 1) * rows] = q.astype(BF16)
    copies[2].wait()


def attend_body(scale, queries, turned, mine, other, wuv_h, keep, send, wuv, keys, sems):
    heads, lat, vdim = wuv.shape
    rows = keep.shape[0]
    width = heads * vdim
    first = (lax.axis_index("grp") & 1) * heads
    copy = pltpu.make_async_copy(wuv_h.at[pl.ds(first, heads)], wuv, sems.at[0])
    copy.start()
    q, r = queries[...], turned[...]
    n = mine.shape[1]
    keys[:, :n] = mine[...]
    keys[:, n:] = other[...]
    s = jnp.dot(q, keys[:lat], preferred_element_type=F32)
    s = (s + jnp.dot(r, keys[lat:], preferred_element_type=F32)) * scale
    top = jnp.max(s, -1, keepdims=True)
    p = jnp.exp(s - top)
    total = jnp.sum(p, -1, keepdims=True)
    w = lax.dot_general(
        p.astype(BF16), keys[:lat], (((1,), (1,)), ((), ())), preferred_element_type=F32
    )
    w = w * (1.0 / total)
    hi = w.astype(BF16)
    lo = (w - hi.astype(F32)).astype(BF16)
    level = top + jnp.log(total)
    lane = lax.broadcasted_iota(jnp.int32, (rows, LANES), 1)
    lse = jnp.zeros((rows, LANES), F32)
    copy.wait()
    for h in range(heads):
        at = slice(h * rows, (h + 1) * rows)
        v = jnp.dot(jnp.concatenate([hi[at], lo[at]], 0), wuv[h], preferred_element_type=F32)
        v = v[:rows] + v[rows:]
        keep[:, h * vdim : (h + 1) * vdim] = v
        send[:, h * vdim : (h + 1) * vdim] = v.astype(BF16)
        lse = jnp.where(lane == h, level[at], lse)
    keep[:, width:] = lse
    send[:, width:] = pack_lse(lse, heads)


def merge_body(heads, own, *refs):
    *others, out = refs
    width = out.shape[1]
    vdim = width // heads
    levels = [own[:, width:]] + [unpack_lse(o[:, width:], heads) for o in others]
    top = levels[0]
    for x in levels[1:]:
        top = jnp.maximum(top, x)
    raised = [jnp.exp(x - top) for x in levels]
    total = sum(raised)
    shares = [x / total for x in raised]
    for h in range(heads):
        at = slice(h * vdim, (h + 1) * vdim)
        v = own[:, at] * shares[0][:, h : h + 1]
        for share, o in zip(shares[1:], others):
            v = v + o[:, at].astype(F32) * share[:, h : h + 1]
        out[:, at] = v.astype(BF16)


def head_rows(width, mine):
    core = lax.axis_index("grp") & 1
    return pl.ds(pl.multiple_of((core if mine else 1 - core) * width, width), width)


def project_mine_body(mine, w, out):
    out[...] = jnp.dot(mine[...], w[head_rows(mine.shape[1], True)], preferred_element_type=F32)


def project_body(part, other, routes, scores, w, keep, *refs):
    *sends, info, res, pad = refs
    width = w.shape[1]
    tail = sends[0].shape[1] - LANES
    count, top = routes.shape
    ctx = lax.axis_index("ctx")
    res[...] = part[...] + jnp.dot(
        other[...], w[head_rows(other.shape[1], False)], preferred_element_type=F32
    )

    def block(turn, s):
        owner = ctx ^ (2 * s + turn)
        return res[pl.ds(pl.multiple_of(owner * count, count), count)]

    v = scores[...]
    v = route_factor * v / jnp.sum(v, -1, keepdims=True)
    hi, mid, lo = split3(v)
    pad[...] = jnp.zeros_like(pad)
    for i, x in enumerate((routes[...].astype(F32), hi, mid, lo)):
        pad[:count, i * top : (i + 1) * top] = x
    info[...] = pad[:count]
    wide = pad[...].astype(BF16)
    for s, send in enumerate(sends, 1):
        send[:, :width] = jnp.concatenate([block(0, s), block(1, s)], 0).astype(BF16)
        if tail > width:
            send[:, width:tail] = jnp.zeros((2 * count, tail - width), BF16)
        send[:, tail:] = wide
    keep[:count] = block(0, 0)
    keep[count:] = block(1, 0)


def rest_sum_body(distances, keep, residual, info, *refs):
    *others, own, send = refs
    count = residual.shape[0]
    width = own.shape[1]
    tail = others[0].shape[1] - LANES
    x = keep[...]
    for o in others:
        x = x + o[:, :width].astype(F32)
    own[:count] = x[:count] + residual[...].astype(F32)
    own[count:] = x[count:]
    send[:, :width] = own[...].astype(BF16)
    if tail > width:
        send[:, width:tail] = jnp.zeros((2 * count, tail - width), BF16)
    per = LANES // 32
    tables = {s: o[:, tail:].astype(F32) for s, o in zip(distances, others)}
    tables[0] = jnp.concatenate([info[...], jnp.zeros_like(info)], 0)
    for i in range((len(tables) + per - 1) // per):
        v = tables[i * per]
        for j in range(1, per):
            if i * per + j in tables:
                v = v + pltpu.roll(tables[i * per + j], 32 * j, 1)
        send[:, tail + i * LANES : tail + (i + 1) * LANES] = v.astype(BF16)


def hidden_body(own, other, hidden, moe):
    count, width = hidden.shape
    o = other[:, :width].astype(F32)
    x = own[...] + jnp.concatenate([o[count:], o[:count]], 0)
    hidden[...] = x[:count]
    moe[...] = x.astype(BF16)


def route_body(local_experts, top, width, mine, other, *refs):
    pick, mix = refs
    count = mine.shape[0] // 2
    far = lax.axis_size("ctx") // 2
    ctx = lax.axis_index("ctx")
    blocks = []
    per = LANES // 32
    for s in range(far):
        at = slice(width + s // per * LANES, width + (s // per + 1) * LANES)
        for ref in (mine, other):
            v = ref[:, at].astype(F32)[:count]
            blocks.append(pltpu.roll(v, (LANES - s % per * 32) % LANES, 1) if s % per else v)
    table = jnp.concatenate(blocks, 0)
    rows = table.shape[0]
    weights = (
        pltpu.roll(table, LANES - top, 1)
        + pltpu.roll(table, LANES - 2 * top, 1)
        + pltpu.roll(table, LANES - 3 * top, 1)
    )
    lane = lax.broadcasted_iota(jnp.int32, (rows, LANES), 1)
    hits, gains = [], []
    all_hits = jnp.zeros((rows, LANES), F32)
    for e in range(local_experts):
        named = (table == (ctx * local_experts + e).astype(F32)) & (lane < top)
        hit = jnp.sum(jnp.where(named, 1.0, 0.0), -1, keepdims=True)
        gains.append(jnp.sum(jnp.where(named, weights, 0.0), -1, keepdims=True))
        hits.append(hit)
        all_hits = jnp.where(lane == e, hit, all_hits)
    a = lax.broadcasted_iota(jnp.int32, (rows, rows), 0)
    b = lax.broadcasted_iota(jnp.int32, (rows, rows), 1)
    earlier = jnp.where((a // count == b // count) & (b < a), 1.0, 0.0).astype(BF16)
    rank = jnp.dot(earlier, all_hits.astype(BF16), preferred_element_type=F32)
    slots = mix.shape[1]
    cap = slots // local_experts
    wide = lax.broadcasted_iota(jnp.int32, (rows, slots), 1)
    start = lax.broadcasted_iota(jnp.int32, (rows, 1), 0) // count * CAP
    chosen = jnp.zeros((rows, slots), F32)
    gain = jnp.zeros((rows, slots), F32)
    for e in range(local_experts):
        slot = rank[:, e : e + 1].astype(jnp.int32) + start + e * cap
        at = (wide == slot) & (hits[e] > 0.5)
        chosen = jnp.where(at, 1.0, chosen)
        gain = jnp.where(at, gains[e], gain)
    pick[...] = jnp.transpose(chosen).astype(BF16)
    mix[...] = gain


def half_cols(hid, mine):
    core = lax.axis_index("grp") & 1
    return pl.ds(pl.multiple_of((core if mine else 1 - core) * hid, hid), hid)


def half_products(experts, mine, x, gate, up, out):
    hid = out.shape[2] // 2
    cap = out.shape[1]
    cols = half_cols(hid, mine)
    for i, e in enumerate(experts):
        xe = x[e * cap : (e + 1) * cap]
        for j, w in enumerate((gate, up)):
            v = jnp.dot(xe, w[e, :, cols], preferred_element_type=F32)
            out[i, :, j * hid : (j + 1) * hid] = v.astype(out.dtype)


def first_half_body(experts, pick, gate, up, *refs):
    *parts, x, send = refs
    rows = jnp.concatenate([p[...] for p in parts], 0)
    x[...] = jnp.dot(pick[...], rows, preferred_element_type=F32).astype(BF16)
    half_products(experts, False, x, gate, up, send)


def half_body(experts, mine, x, gate, up, out):
    half_products(experts, mine, x, gate, up, out)


def own_sum_body(experts, x, gate, up, other, keep, send):
    hid = send.shape[2] // 2
    cap = send.shape[1]
    cols = half_cols(hid, True)
    for i, e in enumerate(experts):
        xe = x[e * cap : (e + 1) * cap]
        for j, w in enumerate((gate, up)):
            at = slice(j * hid, (j + 1) * hid)
            v = jnp.dot(xe, w[e, :, cols], preferred_element_type=F32) + other[e, :, at].astype(F32)
            keep[i, :, at] = v
            send[i, :, at] = v.astype(BF16)


def add_body(experts, x, other, keep, send):
    for i, e in enumerate(experts):
        v = x[i] + other[e].astype(F32)
        keep[i] = v
        send[i] = v.astype(BF16)


def act_body(keep, *refs):
    *others, out = refs
    hid = out.shape[2]
    for i in range(out.shape[0]):
        x = keep[i]
        for o in others:
            x = x + o[i].astype(F32)
        gate, up = x[:, :hid], x[:, hid:]
        out[i] = (gate / (1.0 + jnp.exp(-gate)) * up).astype(BF16)


def weigh(mix, result):
    gain = mix[...]
    rows = gain.shape[0]
    hi = gain.astype(BF16)
    lo = (gain - hi.astype(F32)).astype(BF16)
    v = jnp.dot(jnp.concatenate([hi, lo], 0), result, preferred_element_type=F32)
    return v[:rows] + v[rows:]


def down_mine_body(experts, mine, down, out):
    low = half_cols(mine.shape[2], True)
    for i, e in enumerate(experts):
        out[i] = jnp.dot(mine[i], down[e, low], preferred_element_type=F32)


def down_next_body(experts, later, part, other, mine, down, out, ahead):
    low, high = half_cols(mine.shape[2], True), half_cols(mine.shape[2], False)
    for i, e in enumerate(experts):
        v = part[i] + jnp.dot(other[i], down[e, high], preferred_element_type=F32)
        out[i] = v.astype(BF16)
    for i, e in enumerate(later):
        ahead[i] = jnp.dot(mine[i], down[e, low], preferred_element_type=F32)


def down_last_body(n_before, experts, part, other, down, mix, *refs):
    high = half_cols(other.shape[2], False)
    parts = [r[i] for r in refs[:n_before] for i in range(r.shape[0])]
    for i, e in enumerate(experts):
        v = part[i] + jnp.dot(other[i], down[e, high], preferred_element_type=F32)
        parts.append(v.astype(BF16))
    keep, *sends = refs[n_before:]
    v = weigh(mix, jnp.concatenate(parts, 0))
    n = keep.shape[0]
    keep[...] = v[:n]
    for s, send in enumerate(sends, 1):
        send[...] = v[s * n : (s + 1) * n].astype(BF16)


def last_sum_body(keep, *refs):
    *others, own, send = refs
    count = own.shape[0]
    x = keep[...]
    for o in others:
        x = x + o[...].astype(F32)
    own[...] = x[:count]
    send[...] = x[count:].astype(BF16)


def out_body(hidden, own, other, out):
    out[...] = (hidden[...] + own[...] + other[...].astype(F32)).astype(BF16)


def bind(body, *first):
    def bound(*refs):
        return body(*first, *refs)

    return bound


def per_device(
    q_nope, q_rope, w_uk, w_uv, prompt, w_out, residual, routes, route_scores,
    expert_gate, expert_up, expert_down,
):
    rows, heads, nope = q_nope.shape
    lat, vdim = w_uk.shape[2], w_uv.shape[2]
    n_grp, n_ctx = lax.axis_size("grp"), lax.axis_size("ctx")
    count, width = residual.shape
    top = routes.shape[1]
    experts, _, ff = expert_gate.shape
    cap = CAP * n_ctx
    hid = ff // 2
    hv = heads // 2 * vdim
    tail = -(-width // LANES) * LANES
    far = n_ctx // 2
    in_vmem = lambda a: pltpu.with_memory_space_constraint(a, VMEM)

    keys = prompt.T
    far_keys = swap(keys, "grp", 1)
    many = heads // 2 * rows
    queries, turned, keys = run(
        "queries", query_body,
        [((many, lat), BF16), ((many, q_rope.shape[2]), BF16), (keys.shape, BF16)],
        [q_nope, q_rope, w_uk, keys],
        scratch=[
            VMEM(q_nope.shape, BF16), VMEM(q_rope.shape, BF16), VMEM((heads // 2,) + w_uk.shape[1:], BF16),
            VMEM((heads, rows, nope), BF16), VMEM((heads, rows, q_rope.shape[2]), BF16),
            pltpu.SemaphoreType.DMA((3 + max(1, heads // 8),)),
        ],
        us=2, limit=6, hbm=range(4),
    )
    scale = (nope + q_rope.shape[2]) ** (-0.5)
    keep, send = run(
        "attend", bind(attend_body, scale), [((rows, hv + LANES), F32), ((rows, hv + LANES), BF16)],
        [queries, turned, keys, far_keys, w_uv],
        scratch=[
            VMEM((heads // 2,) + w_uv.shape[1:], BF16), VMEM((keys.shape[0], 2 * keys.shape[1]), BF16),
            pltpu.SemaphoreType.DMA((1,)),
        ],
        us=12, limit=12, hbm=(4,),
    )
    (mine,) = run(
        "merge", bind(merge_body, heads // 2), [((rows, hv), BF16)], [keep] + spread(send, "grp"), us=1
    )
    other = swap(mine, "grp", 1)
    w_out = in_vmem(w_out)
    (part,) = run("project_mine", project_mine_body, [((rows, width), F32)], [mine, w_out], us=0.5)
    pair = 2 * count
    keep, *sends, info = run(
        "project", project_body,
        [((pair, width), F32)] + [((pair, tail + LANES), BF16)] * (far - 1) + [((count, LANES), F32)],
        [part, other, routes, route_scores, w_out],
        scratch=[VMEM((rows, width), F32), VMEM((pair, LANES), F32)], us=1,
    )
    wide = -(-32 * far // LANES) * LANES
    own, send = run(
        "rest_sum", bind(rest_sum_body, list(far_first("ctx"))),
        [((pair, width), F32), ((pair, tail + wide), BF16)],
        [keep, residual, info] + scatter(sends, "ctx"), us=1,
    )
    other = swap(send, "ctx", 1)
    hidden, moe = run(
        "hidden", hidden_body, [((count, width), F32), ((pair, width), BF16)], [own, other], us=1
    )
    parts = dict(zip(far_first("ctx"), spread(moe, "ctx")))
    parts[0] = moe
    pick, mix = run(
        "route", bind(route_body, experts, top, tail),
        [((experts * cap, rows), BF16), ((rows, experts * cap), F32)], [send, other], us=0.5, after=[parts[far - 1]],
    )
    gate, up, down = in_vmem(expert_gate), in_vmem(expert_up), in_vmem(expert_down)
    size = -(-experts // 2)
    groups = [range(i, i + size) for i in range(0, experts, size)]
    shape = (size, cap, 2 * hid)
    whole = (experts, cap, 2 * hid)
    x, send = run(
        "other_half", bind(first_half_body, range(experts)),
        [((experts * cap, width), BF16), (whole, BF16)],
        [pick, gate, up] + [parts[s] for s in range(far)], us=0.5,
    )
    other = swap(send, "grp", 1)
    sums = []
    for g in groups:
        if sums:
            keep, send = run(
                "own_sum", bind(own_sum_body, g), [(shape, F32), (shape, BF16)],
                [x, gate, up, other], us=0.5, after=[sums[-1][0]],
            )
        else:
            (part,) = run(
                "own_half", bind(half_body, g, True), [(shape, F32)], [x, gate, up], us=0.5, after=[send]
            )
            keep, send = run(
                "add", bind(add_body, g), [(shape, F32), (shape, BF16)], [part, other], us=0.1
            )
        sums.append((keep, spread(send, "grp")))
    before, later = [], []
    for g, (keep, others) in zip(groups, sums):
        (act,) = run(
            "act", act_body, [((size, cap, hid), BF16)], [keep] + others, us=5,
            after=later or [sums[-1][0]],
        )
        other_act = swap(act, "grp", 1)
        if later:
            before, part = run(
                "down_next", bind(down_next_body, groups[0], g),
                [((size, cap, width), BF16), ((size, cap, width), F32)],
                [later[0], last_act, act, down], us=1,
            )
            before = [before]
        else:
            (part,) = run(
                "down_mine", bind(down_mine_body, g), [((size, cap, width), F32)], [act, down], us=0.5
            )
            later, last_act = [part], other_act
    keep, *sends = run(
        "down_last", bind(down_last_body, len(before), groups[-1]),
        [((pair, width), F32)] + [((pair, width), BF16)] * (far - 1),
        [part, other_act, down, mix] + before, us=1,
    )
    own, send = run(
        "last_sum", last_sum_body, [((count, width), F32), ((count, width), BF16)],
        [keep] + scatter(sends, "ctx"), us=3,
    )
    (out,) = run(
        "out", out_body, [((count, width), BF16)], [hidden, own, swap(send, "ctx", 1)], us=1
    )
    return out


def solution(mesh):
    in_specs = (
        P(None, "ctx", None),
        P(None, "ctx", None),
        P("ctx", None, None),
        P("ctx", None, None),
        P("grp", None),
        P("ctx", "grp"),
        P("ctx", "grp"),
        P("ctx", None),
        P("ctx", None),
        P("ctx", "grp", None),
        P("ctx", "grp", None),
        P("ctx", None, "grp"),
    )
    return jax.shard_map(
        per_device, mesh=mesh, in_specs=in_specs, out_specs=P("ctx", "grp"), check_vma=False
    )
```

```python
import jax
import jax.numpy as jnp
from jax import lax
from jax.experimental import pallas as pl
from jax.experimental.pallas import tpu as pltpu
from jax.sharding import PartitionSpec as P

CAP = 4
LANES = 128
route_factor = 2.5
F32 = jnp.float32
BF16 = jnp.bfloat16
VMEM = pltpu.VMEM


def swap(x, axis, bits):
    return lax.ppermute(x, axis, [(a, a ^ bits) for a in range(lax.axis_size(axis))])


def far_first(axis):
    return range(lax.axis_size(axis) // 2 - 1, 0, -1)


def spread(x, axis):
    return [swap(x, axis, 2 * s) for s in far_first(axis)]


def scatter(parts, axis):
    return [swap(parts[s - 1], axis, 2 * s) for s in far_first(axis)]


def run(name, body, outs, ins, scratch=(), us=1.0, limit=3, hbm=(), after=()):
    n_ins, n_after = len(ins), len(after)
    ins = [
        pltpu.with_memory_space_constraint(a, pltpu.HBM) if i in hbm else a
        for i, a in enumerate(ins)
    ]

    def ordered(*refs):
        return body(*refs[:n_ins], *refs[n_ins + n_after :])

    return pl.pallas_call(
        ordered,
        out_shape=[jax.ShapeDtypeStruct(s, d) for s, d in outs],
        in_specs=[
            pl.BlockSpec(memory_space=pltpu.HBM if i in hbm else VMEM) for i in range(n_ins)
        ]
        + [pl.BlockSpec(memory_space=pl.ANY)] * n_after,
        out_specs=[pl.BlockSpec(memory_space=VMEM) for _ in outs],
        scratch_shapes=list(scratch),
        cost_estimate=pl.CostEstimate(
            flops=int(us * 1.15e9), bytes_accessed=1024, transcendentals=0
        ),
        compiler_params=pltpu.CompilerParams(vmem_limit_bytes=limit << 20),
        name=name,
    )(*ins, *after)


def split3(x):
    hi = x.astype(BF16).astype(F32)
    mid = (x - hi).astype(BF16).astype(F32)
    return hi, mid, x - hi - mid


def pack_lse(x, heads):
    hi, mid, lo = split3(x)
    return (hi + pltpu.roll(mid, heads, 1) + pltpu.roll(lo, 2 * heads, 1)).astype(BF16)


def unpack_lse(x, heads):
    x = x.astype(F32)
    x = x + pltpu.roll(x, LANES - heads, 1) + pltpu.roll(x, LANES - 2 * heads, 1)
    lane = lax.broadcasted_iota(jnp.int32, x.shape, 1)
    return jnp.where(lane < heads, x, 0.0)


def query_body(qn_h, qr_h, wuk_h, keys_h, queries, turned, keys, qn, qr, wuk, nope_scr, rope_scr, sems):
    rows, heads, _ = qn.shape
    half = heads // 2
    group = min(4, half)
    steps = half // group
    first = (lax.axis_index("grp") & 1) * half
    copies = [
        pltpu.make_async_copy(qn_h, qn, sems.at[0]),
        pltpu.make_async_copy(qr_h, qr, sems.at[1]),
        pltpu.make_async_copy(keys_h, keys, sems.at[2]),
    ]
    uk = [
        pltpu.make_async_copy(
            wuk_h.at[pl.ds(first + c * group, group)], wuk.at[pl.ds(c * group, group)], sems.at[3 + c]
        )
        for c in range(steps)
    ]
    for copy in [copies[0], uk[0], copies[1]] + uk[1:] + [copies[2]]:
        copy.start()
    copies[0].wait()
    nope_scr[...] = jnp.swapaxes(qn[...], 0, 1)
    copies[1].wait()
    rope_scr[...] = jnp.swapaxes(qr[...], 0, 1)
    for h in range(half):
        turned[h * rows : (h + 1) * rows] = rope_scr[first + h]
        if h % group == 0:
            uk[h // group].wait()
        q = jnp.dot(nope_scr[first + h], wuk[h], preferred_element_type=F32)
        queries[h * rows : (h + 1) * rows] = q.astype(BF16)
    copies[2].wait()


def attend_body(scale, queries, turned, mine, other, wuv_h, keep, send, wuv, keys, sems):
    heads, lat, vdim = wuv.shape
    rows = keep.shape[0]
    width = heads * vdim
    first = (lax.axis_index("grp") & 1) * heads
    copy = pltpu.make_async_copy(wuv_h.at[pl.ds(first, heads)], wuv, sems.at[0])
    copy.start()
    q, r = queries[...], turned[...]
    n = mine.shape[1]
    keys[:, :n] = mine[...]
    keys[:, n:] = other[...]
    s = jnp.dot(q, keys[:lat], preferred_element_type=F32)
    s = (s + jnp.dot(r, keys[lat:], preferred_element_type=F32)) * scale
    top = jnp.max(s, -1, keepdims=True)
    p = jnp.exp(s - top)
    total = jnp.sum(p, -1, keepdims=True)
    w = lax.dot_general(
        p.astype(BF16), keys[:lat], (((1,), (1,)), ((), ())), preferred_element_type=F32
    )
    w = w.astype(BF16)
    share = 1.0 / total
    level = top + jnp.log(total)
    lane = lax.broadcasted_iota(jnp.int32, (rows, LANES), 1)
    lse = jnp.zeros((rows, LANES), F32)
    copy.wait()
    for h in range(heads):
        at = slice(h * rows, (h + 1) * rows)
        v = jnp.dot(w[at], wuv[h], preferred_element_type=F32) * share[at]
        keep[:, h * vdim : (h + 1) * vdim] = v
        send[:, h * vdim : (h + 1) * vdim] = v.astype(BF16)
        lse = jnp.where(lane == h, level[at], lse)
    keep[:, width:] = lse
    send[:, width:] = pack_lse(lse, heads)


def merge_body(heads, own, *refs):
    *others, out = refs
    width = out.shape[1]
    vdim = width // heads
    levels = [own[:, width:]] + [unpack_lse(o[:, width:], heads) for o in others]
    top = levels[0]
    for x in levels[1:]:
        top = jnp.maximum(top, x)
    raised = [jnp.exp(x - top) for x in levels]
    total = sum(raised)
    shares = [x / total for x in raised]
    for h in range(heads):
        at = slice(h * vdim, (h + 1) * vdim)
        v = own[:, at] * shares[0][:, h : h + 1]
        for share, o in zip(shares[1:], others):
            v = v + o[:, at].astype(F32) * share[:, h : h + 1]
        out[:, at] = v.astype(BF16)


def head_rows(width, mine):
    core = lax.axis_index("grp") & 1
    return pl.ds(pl.multiple_of((core if mine else 1 - core) * width, width), width)


def project_mine_body(mine, w, out):
    out[...] = jnp.dot(mine[...], w[head_rows(mine.shape[1], True)], preferred_element_type=F32)


def project_body(part, other, routes, scores, w, keep, *refs):
    *sends, info, res, pad = refs
    width = w.shape[1]
    tail = sends[0].shape[1] - LANES
    count, top = routes.shape
    ctx = lax.axis_index("ctx")
    res[...] = part[...] + jnp.dot(
        other[...], w[head_rows(other.shape[1], False)], preferred_element_type=F32
    )

    def block(turn, s):
        owner = ctx ^ (2 * s + turn)
        return res[pl.ds(pl.multiple_of(owner * count, count), count)]

    v = scores[...]
    v = route_factor * v / jnp.sum(v, -1, keepdims=True)
    hi, mid, lo = split3(v)
    pad[...] = jnp.zeros_like(pad)
    for i, x in enumerate((routes[...].astype(F32), hi, mid, lo)):
        pad[:count, i * top : (i + 1) * top] = x
    info[...] = pad[:count]
    wide = pad[...].astype(BF16)
    for s, send in enumerate(sends, 1):
        send[:, :width] = jnp.concatenate([block(0, s), block(1, s)], 0).astype(BF16)
        if tail > width:
            send[:, width:tail] = jnp.zeros((2 * count, tail - width), BF16)
        send[:, tail:] = wide
    keep[:count] = block(0, 0)
    keep[count:] = block(1, 0)


def rest_sum_body(distances, keep, residual, info, *refs):
    *others, own, send = refs
    count = residual.shape[0]
    width = own.shape[1]
    tail = others[0].shape[1] - LANES
    x = keep[...]
    for o in others:
        x = x + o[:, :width].astype(F32)
    own[:count] = x[:count] + residual[...].astype(F32)
    own[count:] = x[count:]
    send[:, :width] = own[...].astype(BF16)
    if tail > width:
        send[:, width:tail] = jnp.zeros((2 * count, tail - width), BF16)
    per = LANES // 32
    tables = {s: o[:, tail:].astype(F32) for s, o in zip(distances, others)}
    tables[0] = jnp.concatenate([info[...], jnp.zeros_like(info)], 0)
    for i in range((len(tables) + per - 1) // per):
        v = tables[i * per]
        for j in range(1, per):
            if i * per + j in tables:
                v = v + pltpu.roll(tables[i * per + j], 32 * j, 1)
        send[:, tail + i * LANES : tail + (i + 1) * LANES] = v.astype(BF16)


def hidden_body(own, other, hidden, moe):
    count, width = hidden.shape
    o = other[:, :width].astype(F32)
    x = own[...] + jnp.concatenate([o[count:], o[:count]], 0)
    hidden[...] = x[:count]
    moe[...] = x.astype(BF16)


def route_body(local_experts, top, width, mine, other, *refs):
    pick, mix = refs
    count = mine.shape[0] // 2
    far = lax.axis_size("ctx") // 2
    ctx = lax.axis_index("ctx")
    blocks = []
    per = LANES // 32
    for s in range(far):
        at = slice(width + s // per * LANES, width + (s // per + 1) * LANES)
        for ref in (mine, other):
            v = ref[:, at].astype(F32)[:count]
            blocks.append(pltpu.roll(v, (LANES - s % per * 32) % LANES, 1) if s % per else v)
    table = jnp.concatenate(blocks, 0)
    rows = table.shape[0]
    weights = (
        pltpu.roll(table, LANES - top, 1)
        + pltpu.roll(table, LANES - 2 * top, 1)
        + pltpu.roll(table, LANES - 3 * top, 1)
    )
    lane = lax.broadcasted_iota(jnp.int32, (rows, LANES), 1)
    hits, gains = [], []
    all_hits = jnp.zeros((rows, LANES), F32)
    for e in range(local_experts):
        named = (table == (ctx * local_experts + e).astype(F32)) & (lane < top)
        hit = jnp.sum(jnp.where(named, 1.0, 0.0), -1, keepdims=True)
        gains.append(jnp.sum(jnp.where(named, weights, 0.0), -1, keepdims=True))
        hits.append(hit)
        all_hits = jnp.where(lane == e, hit, all_hits)
    a = lax.broadcasted_iota(jnp.int32, (rows, rows), 0)
    b = lax.broadcasted_iota(jnp.int32, (rows, rows), 1)
    earlier = jnp.where((a // count == b // count) & (b < a), 1.0, 0.0).astype(BF16)
    rank = jnp.dot(earlier, all_hits.astype(BF16), preferred_element_type=F32)
    slots = mix.shape[1]
    cap = slots // local_experts
    wide = lax.broadcasted_iota(jnp.int32, (rows, slots), 1)
    start = lax.broadcasted_iota(jnp.int32, (rows, 1), 0) // count * CAP
    chosen = jnp.zeros((rows, slots), F32)
    gain = jnp.zeros((rows, slots), F32)
    for e in range(local_experts):
        slot = rank[:, e : e + 1].astype(jnp.int32) + start + e * cap
        at = (wide == slot) & (hits[e] > 0.5)
        chosen = jnp.where(at, 1.0, chosen)
        gain = jnp.where(at, gains[e], gain)
    pick[...] = jnp.transpose(chosen).astype(BF16)
    mix[...] = gain


def half_cols(hid, mine):
    core = lax.axis_index("grp") & 1
    return pl.ds(pl.multiple_of((core if mine else 1 - core) * hid, hid), hid)


def half_products(experts, mine, x, gate, up, out):
    hid = out.shape[2] // 2
    cap = out.shape[1]
    cols = half_cols(hid, mine)
    for i, e in enumerate(experts):
        xe = x[e * cap : (e + 1) * cap]
        for j, w in enumerate((gate, up)):
            v = jnp.dot(xe, w[e, :, cols], preferred_element_type=F32)
            out[i, :, j * hid : (j + 1) * hid] = v.astype(out.dtype)


def first_half_body(experts, pick, gate, up, *refs):
    *parts, x, send = refs
    rows = jnp.concatenate([p[...] for p in parts], 0)
    x[...] = jnp.dot(pick[...], rows, preferred_element_type=F32).astype(BF16)
    half_products(experts, False, x, gate, up, send)


def half_body(experts, mine, x, gate, up, out):
    half_products(experts, mine, x, gate, up, out)


def own_sum_body(experts, x, gate, up, other, keep, send):
    hid = send.shape[2] // 2
    cap = send.shape[1]
    cols = half_cols(hid, True)
    for i, e in enumerate(experts):
        xe = x[e * cap : (e + 1) * cap]
        for j, w in enumerate((gate, up)):
            at = slice(j * hid, (j + 1) * hid)
            v = jnp.dot(xe, w[e, :, cols], preferred_element_type=F32) + other[e, :, at].astype(F32)
            keep[i, :, at] = v
            send[i, :, at] = v.astype(BF16)


def add_body(experts, x, other, keep, send):
    for i, e in enumerate(experts):
        v = x[i] + other[e].astype(F32)
        keep[i] = v
        send[i] = v.astype(BF16)


def act_body(keep, *refs):
    *others, out = refs
    hid = out.shape[2]
    for i in range(out.shape[0]):
        x = keep[i]
        for o in others:
            x = x + o[i].astype(F32)
        gate, up = x[:, :hid], x[:, hid:]
        out[i] = (gate / (1.0 + jnp.exp(-gate)) * up).astype(BF16)


def weigh(mix, result):
    gain = mix[...]
    rows = gain.shape[0]
    hi = gain.astype(BF16)
    lo = (gain - hi.astype(F32)).astype(BF16)
    v = jnp.dot(jnp.concatenate([hi, lo], 0), result, preferred_element_type=F32)
    return v[:rows] + v[rows:]


def down_mine_body(experts, mine, down, out):
    low = half_cols(mine.shape[2], True)
    for i, e in enumerate(experts):
        out[i] = jnp.dot(mine[i], down[e, low], preferred_element_type=F32)


def down_next_body(experts, later, part, other, mine, down, out, ahead):
    low, high = half_cols(mine.shape[2], True), half_cols(mine.shape[2], False)
    for i, e in enumerate(experts):
        v = part[i] + jnp.dot(other[i], down[e, high], preferred_element_type=F32)
        out[i] = v.astype(BF16)
    for i, e in enumerate(later):
        ahead[i] = jnp.dot(mine[i], down[e, low], preferred_element_type=F32)


def down_last_body(n_before, experts, part, other, down, mix, *refs):
    high = half_cols(other.shape[2], False)
    parts = [r[i] for r in refs[:n_before] for i in range(r.shape[0])]
    for i, e in enumerate(experts):
        v = part[i] + jnp.dot(other[i], down[e, high], preferred_element_type=F32)
        parts.append(v.astype(BF16))
    keep, *sends = refs[n_before:]
    v = weigh(mix, jnp.concatenate(parts, 0))
    n = keep.shape[0]
    keep[...] = v[:n]
    for s, send in enumerate(sends, 1):
        send[...] = v[s * n : (s + 1) * n].astype(BF16)


def last_sum_body(keep, *refs):
    *others, own, send = refs
    count = own.shape[0]
    x = keep[...]
    for o in others:
        x = x + o[...].astype(F32)
    own[...] = x[:count]
    send[...] = x[count:].astype(BF16)


def out_body(hidden, own, other, out):
    out[...] = (hidden[...] + own[...] + other[...].astype(F32)).astype(BF16)


def bind(body, *first):
    def bound(*refs):
        return body(*first, *refs)

    return bound


def per_device(
    q_nope, q_rope, w_uk, w_uv, prompt, w_out, residual, routes, route_scores,
    expert_gate, expert_up, expert_down,
):
    rows, heads, nope = q_nope.shape
    lat, vdim = w_uk.shape[2], w_uv.shape[2]
    n_grp, n_ctx = lax.axis_size("grp"), lax.axis_size("ctx")
    count, width = residual.shape
    top = routes.shape[1]
    experts, _, ff = expert_gate.shape
    cap = CAP * n_ctx
    hid = ff // 2
    hv = heads // 2 * vdim
    tail = -(-width // LANES) * LANES
    far = n_ctx // 2
    in_vmem = lambda a: pltpu.with_memory_space_constraint(a, VMEM)

    keys = prompt.T
    far_keys = swap(keys, "grp", 1)
    many = heads // 2 * rows
    queries, turned, keys = run(
        "queries", query_body,
        [((many, lat), BF16), ((many, q_rope.shape[2]), BF16), (keys.shape, BF16)],
        [q_nope, q_rope, w_uk, keys],
        scratch=[
            VMEM(q_nope.shape, BF16), VMEM(q_rope.shape, BF16), VMEM((heads // 2,) + w_uk.shape[1:], BF16),
            VMEM((heads, rows, nope), BF16), VMEM((heads, rows, q_rope.shape[2]), BF16),
            pltpu.SemaphoreType.DMA((3 + max(1, heads // 8),)),
        ],
        us=2, limit=6, hbm=range(4),
    )
    scale = (nope + q_rope.shape[2]) ** (-0.5)
    keep, send = run(
        "attend", bind(attend_body, scale), [((rows, hv + LANES), F32), ((rows, hv + LANES), BF16)],
        [queries, turned, keys, far_keys, w_uv],
        scratch=[
            VMEM((heads // 2,) + w_uv.shape[1:], BF16), VMEM((keys.shape[0], 2 * keys.shape[1]), BF16),
            pltpu.SemaphoreType.DMA((1,)),
        ],
        us=12, limit=12, hbm=(4,),
    )
    (mine,) = run(
        "merge", bind(merge_body, heads // 2), [((rows, hv), BF16)], [keep] + spread(send, "grp"), us=1
    )
    other = swap(mine, "grp", 1)
    w_out = in_vmem(w_out)
    (part,) = run("project_mine", project_mine_body, [((rows, width), F32)], [mine, w_out], us=0.5)
    pair = 2 * count
    keep, *sends, info = run(
        "project", project_body,
        [((pair, width), F32)] + [((pair, tail + LANES), BF16)] * (far - 1) + [((count, LANES), F32)],
        [part, other, routes, route_scores, w_out],
        scratch=[VMEM((rows, width), F32), VMEM((pair, LANES), F32)], us=1,
    )
    wide = -(-32 * far // LANES) * LANES
    own, send = run(
        "rest_sum", bind(rest_sum_body, list(far_first("ctx"))),
        [((pair, width), F32), ((pair, tail + wide), BF16)],
        [keep, residual, info] + scatter(sends, "ctx"), us=1,
    )
    other = swap(send, "ctx", 1)
    hidden, moe = run(
        "hidden", hidden_body, [((count, width), F32), ((pair, width), BF16)], [own, other], us=1
    )
    parts = dict(zip(far_first("ctx"), spread(moe, "ctx")))
    parts[0] = moe
    pick, mix = run(
        "route", bind(route_body, experts, top, tail),
        [((experts * cap, rows), BF16), ((rows, experts * cap), F32)], [send, other], us=0.5, after=[parts[far - 1]],
    )
    gate, up, down = in_vmem(expert_gate), in_vmem(expert_up), in_vmem(expert_down)
    size = -(-experts // 2)
    groups = [range(i, i + size) for i in range(0, experts, size)]
    shape = (size, cap, 2 * hid)
    whole = (experts, cap, 2 * hid)
    x, send = run(
        "other_half", bind(first_half_body, range(experts)),
        [((experts * cap, width), BF16), (whole, BF16)],
        [pick, gate, up] + [parts[s] for s in range(far)], us=0.5,
    )
    other = swap(send, "grp", 1)
    sums = []
    for g in groups:
        (part,) = run(
            "own_half", bind(half_body, g, True), [(shape, F32)], [x, gate, up], us=5 if sums else 0.5,
            after=[sums[-1][0] if sums else send],
        )
        keep, send = run(
            "add", bind(add_body, g), [(shape, F32), (shape, BF16)], [part, other],
            us=1 if sums else 0.1,
        )
        sums.append((keep, spread(send, "grp")))
    before, later = [], []
    for g, (keep, others) in zip(groups, sums):
        (act,) = run(
            "act", act_body, [((size, cap, hid), BF16)], [keep] + others, us=1.5,
            after=later or [sums[-1][0]],
        )
        other_act = swap(act, "grp", 1)
        if later:
            before, part = run(
                "down_next", bind(down_next_body, groups[0], g),
                [((size, cap, width), BF16), ((size, cap, width), F32)],
                [later[0], last_act, act, down], us=1,
            )
            before = [before]
        else:
            (part,) = run(
                "down_mine", bind(down_mine_body, g), [((size, cap, width), F32)], [act, down], us=0.5
            )
            later, last_act = [part], other_act
    keep, *sends = run(
        "down_last", bind(down_last_body, len(before), groups[-1]),
        [((pair, width), F32)] + [((pair, width), BF16)] * (far - 1),
        [part, other_act, down, mix] + before, us=1,
    )
    own, send = run(
        "last_sum", last_sum_body, [((count, width), F32), ((count, width), BF16)],
        [keep] + scatter(sends, "ctx"), us=3,
    )
    (out,) = run(
        "out", out_body, [((count, width), BF16)], [hidden, own, swap(send, "ctx", 1)], us=1
    )
    return out


def solution(mesh):
    in_specs = (
        P(None, "ctx", None),
        P(None, "ctx", None),
        P("ctx", None, None),
        P("ctx", None, None),
        P("grp", None),
        P("ctx", "grp"),
        P("ctx", "grp"),
        P("ctx", None),
        P("ctx", None),
        P("ctx", "grp", None),
        P("ctx", "grp", None),
        P("ctx", None, "grp"),
    )
    return jax.shard_map(
        per_device, mesh=mesh, in_specs=in_specs, out_specs=P("ctx", "grp"), check_vma=False
    )
```

```python
import jax
import jax.numpy as jnp
from jax import lax
from jax.experimental import pallas as pl
from jax.experimental.pallas import tpu as pltpu
from jax.sharding import PartitionSpec as P

CAP = 4
LANES = 128
route_factor = 2.5
F32 = jnp.float32
BF16 = jnp.bfloat16
VMEM = pltpu.VMEM


def swap(x, axis, bits):
    return lax.ppermute(x, axis, [(a, a ^ bits) for a in range(lax.axis_size(axis))])


def far_first(axis):
    return range(lax.axis_size(axis) // 2 - 1, 0, -1)


def spread(x, axis):
    return [swap(x, axis, 2 * s) for s in far_first(axis)]


def scatter(parts, axis):
    return [swap(parts[s - 1], axis, 2 * s) for s in far_first(axis)]


def run(name, body, outs, ins, scratch=(), us=1.0, limit=3, hbm=(), after=()):
    n_ins, n_after = len(ins), len(after)
    ins = [
        pltpu.with_memory_space_constraint(a, pltpu.HBM) if i in hbm else a
        for i, a in enumerate(ins)
    ]

    def ordered(*refs):
        return body(*refs[:n_ins], *refs[n_ins + n_after :])

    return pl.pallas_call(
        ordered,
        out_shape=[jax.ShapeDtypeStruct(s, d) for s, d in outs],
        in_specs=[
            pl.BlockSpec(memory_space=pltpu.HBM if i in hbm else VMEM) for i in range(n_ins)
        ]
        + [pl.BlockSpec(memory_space=pl.ANY)] * n_after,
        out_specs=[pl.BlockSpec(memory_space=VMEM) for _ in outs],
        scratch_shapes=list(scratch),
        cost_estimate=pl.CostEstimate(
            flops=int(us * 1.15e9), bytes_accessed=1024, transcendentals=0
        ),
        compiler_params=pltpu.CompilerParams(vmem_limit_bytes=limit << 20),
        name=name,
    )(*ins, *after)


def split3(x):
    hi = x.astype(BF16).astype(F32)
    mid = (x - hi).astype(BF16).astype(F32)
    return hi, mid, x - hi - mid


def pack_lse(x, heads):
    hi, mid, lo = split3(x)
    return (hi + pltpu.roll(mid, heads, 1) + pltpu.roll(lo, 2 * heads, 1)).astype(BF16)


def unpack_lse(x, heads):
    x = x.astype(F32)
    x = x + pltpu.roll(x, LANES - heads, 1) + pltpu.roll(x, LANES - 2 * heads, 1)
    lane = lax.broadcasted_iota(jnp.int32, x.shape, 1)
    return jnp.where(lane < heads, x, 0.0)


def query_body(qn_h, qr_h, wuk_h, keys_h, queries, turned, keys, qn, qr, wuk, nope_scr, rope_scr, sems):
    rows, heads, _ = qn.shape
    half = heads // 2
    group = min(8, half)
    steps = half // group
    first = (lax.axis_index("grp") & 1) * half
    copies = [
        pltpu.make_async_copy(qn_h, qn, sems.at[0]),
        pltpu.make_async_copy(qr_h, qr, sems.at[1]),
        pltpu.make_async_copy(keys_h, keys, sems.at[2]),
    ]
    uk = [
        pltpu.make_async_copy(
            wuk_h.at[pl.ds(first + c * group, group)], wuk.at[pl.ds(c * group, group)], sems.at[3 + c]
        )
        for c in range(steps)
    ]
    for copy in [copies[0], uk[0], copies[1]] + uk[1:] + [copies[2]]:
        copy.start()
    copies[0].wait()
    nope_scr[...] = jnp.swapaxes(qn[...], 0, 1)
    copies[1].wait()
    rope_scr[...] = jnp.swapaxes(qr[...], 0, 1)
    for h in range(half):
        turned[h * rows : (h + 1) * rows] = rope_scr[first + h]
        if h % group == 0:
            uk[h // group].wait()
        q = jnp.dot(nope_scr[first + h], wuk[h], preferred_element_type=F32)
        queries[h * rows : (h + 1) * rows] = q.astype(BF16)
    copies[2].wait()


def attend_body(scale, queries, turned, mine, other, wuv_h, keep, send, wuv, keys, sems):
    heads, lat, vdim = wuv.shape
    rows = keep.shape[0]
    width = heads * vdim
    first = (lax.axis_index("grp") & 1) * heads
    copy = pltpu.make_async_copy(wuv_h.at[pl.ds(first, heads)], wuv, sems.at[0])
    copy.start()
    q, r = queries[...], turned[...]
    n = mine.shape[1]
    keys[:, :n] = mine[...]
    keys[:, n:] = other[...]
    s = jnp.dot(q, keys[:lat], preferred_element_type=F32)
    s = (s + jnp.dot(r, keys[lat:], preferred_element_type=F32)) * scale
    top = jnp.max(s, -1, keepdims=True)
    p = jnp.exp(s - top)
    total = jnp.sum(p, -1, keepdims=True)
    w = lax.dot_general(
        p.astype(BF16), keys[:lat], (((1,), (1,)), ((), ())), preferred_element_type=F32
    )
    w = w * (1.0 / total)
    hi = w.astype(BF16)
    lo = (w - hi.astype(F32)).astype(BF16)
    level = top + jnp.log(total)
    lane = lax.broadcasted_iota(jnp.int32, (rows, LANES), 1)
    lse = jnp.zeros((rows, LANES), F32)
    copy.wait()
    for h in range(heads):
        at = slice(h * rows, (h + 1) * rows)
        v = jnp.dot(jnp.concatenate([hi[at], lo[at]], 0), wuv[h], preferred_element_type=F32)
        v = v[:rows] + v[rows:]
        keep[:, h * vdim : (h + 1) * vdim] = v
        send[:, h * vdim : (h + 1) * vdim] = v.astype(BF16)
        lse = jnp.where(lane == h, level[at], lse)
    keep[:, width:] = lse
    send[:, width:] = pack_lse(lse, heads)


def merge_body(heads, own, *refs):
    *others, out = refs
    width = out.shape[1]
    vdim = width // heads
    levels = [own[:, width:]] + [unpack_lse(o[:, width:], heads) for o in others]
    top = levels[0]
    for x in levels[1:]:
        top = jnp.maximum(top, x)
    raised = [jnp.exp(x - top) for x in levels]
    total = sum(raised)
    shares = [x / total for x in raised]
    for h in range(heads):
        at = slice(h * vdim, (h + 1) * vdim)
        v = own[:, at] * shares[0][:, h : h + 1]
        for share, o in zip(shares[1:], others):
            v = v + o[:, at].astype(F32) * share[:, h : h + 1]
        out[:, at] = v.astype(BF16)


def head_rows(width, mine):
    core = lax.axis_index("grp") & 1
    return pl.ds(pl.multiple_of((core if mine else 1 - core) * width, width), width)


def project_mine_body(mine, w, out):
    out[...] = jnp.dot(mine[...], w[head_rows(mine.shape[1], True)], preferred_element_type=F32)


def project_body(part, other, routes, scores, w, keep, *refs):
    *sends, info, res, pad = refs
    width = w.shape[1]
    tail = sends[0].shape[1] - LANES
    count, top = routes.shape
    ctx = lax.axis_index("ctx")
    res[...] = part[...] + jnp.dot(
        other[...], w[head_rows(other.shape[1], False)], preferred_element_type=F32
    )

    def block(turn, s):
        owner = ctx ^ (2 * s + turn)
        return res[pl.ds(pl.multiple_of(owner * count, count), count)]

    v = scores[...]
    v = route_factor * v / jnp.sum(v, -1, keepdims=True)
    hi, mid, lo = split3(v)
    pad[...] = jnp.zeros_like(pad)
    for i, x in enumerate((routes[...].astype(F32), hi, mid, lo)):
        pad[:count, i * top : (i + 1) * top] = x
    info[...] = pad[:count]
    wide = pad[...].astype(BF16)
    for s, send in enumerate(sends, 1):
        send[:, :width] = jnp.concatenate([block(0, s), block(1, s)], 0).astype(BF16)
        if tail > width:
            send[:, width:tail] = jnp.zeros((2 * count, tail - width), BF16)
        send[:, tail:] = wide
    keep[:count] = block(0, 0)
    keep[count:] = block(1, 0)


def rest_sum_body(distances, keep, residual, info, *refs):
    *others, own, send = refs
    count = residual.shape[0]
    width = own.shape[1]
    tail = others[0].shape[1] - LANES
    x = keep[...]
    for o in others:
        x = x + o[:, :width].astype(F32)
    own[:count] = x[:count] + residual[...].astype(F32)
    own[count:] = x[count:]
    send[:, :width] = own[...].astype(BF16)
    if tail > width:
        send[:, width:tail] = jnp.zeros((2 * count, tail - width), BF16)
    per = LANES // 32
    tables = {s: o[:, tail:].astype(F32) for s, o in zip(distances, others)}
    tables[0] = jnp.concatenate([info[...], jnp.zeros_like(info)], 0)
    for i in range((len(tables) + per - 1) // per):
        v = tables[i * per]
        for j in range(1, per):
            if i * per + j in tables:
                v = v + pltpu.roll(tables[i * per + j], 32 * j, 1)
        send[:, tail + i * LANES : tail + (i + 1) * LANES] = v.astype(BF16)


def hidden_body(own, other, hidden, moe):
    count, width = hidden.shape
    o = other[:, :width].astype(F32)
    x = own[...] + jnp.concatenate([o[count:], o[:count]], 0)
    hidden[...] = x[:count]
    moe[...] = x.astype(BF16)


def route_body(local_experts, top, width, mine, other, *refs):
    pick, mix = refs
    count = mine.shape[0] // 2
    far = lax.axis_size("ctx") // 2
    ctx = lax.axis_index("ctx")
    blocks = []
    per = LANES // 32
    for s in range(far):
        at = slice(width + s // per * LANES, width + (s // per + 1) * LANES)
        for ref in (mine, other):
            v = ref[:, at].astype(F32)[:count]
            blocks.append(pltpu.roll(v, (LANES - s % per * 32) % LANES, 1) if s % per else v)
    table = jnp.concatenate(blocks, 0)
    rows = table.shape[0]
    weights = (
        pltpu.roll(table, LANES - top, 1)
        + pltpu.roll(table, LANES - 2 * top, 1)
        + pltpu.roll(table, LANES - 3 * top, 1)
    )
    lane = lax.broadcasted_iota(jnp.int32, (rows, LANES), 1)
    hits, gains = [], []
    all_hits = jnp.zeros((rows, LANES), F32)
    for e in range(local_experts):
        named = (table == (ctx * local_experts + e).astype(F32)) & (lane < top)
        hit = jnp.sum(jnp.where(named, 1.0, 0.0), -1, keepdims=True)
        gains.append(jnp.sum(jnp.where(named, weights, 0.0), -1, keepdims=True))
        hits.append(hit)
        all_hits = jnp.where(lane == e, hit, all_hits)
    a = lax.broadcasted_iota(jnp.int32, (rows, rows), 0)
    b = lax.broadcasted_iota(jnp.int32, (rows, rows), 1)
    earlier = jnp.where((a // count == b // count) & (b < a), 1.0, 0.0).astype(BF16)
    rank = jnp.dot(earlier, all_hits.astype(BF16), preferred_element_type=F32)
    slots = mix.shape[1]
    cap = slots // local_experts
    wide = lax.broadcasted_iota(jnp.int32, (rows, slots), 1)
    start = lax.broadcasted_iota(jnp.int32, (rows, 1), 0) // count * CAP
    chosen = jnp.zeros((rows, slots), F32)
    gain = jnp.zeros((rows, slots), F32)
    for e in range(local_experts):
        slot = rank[:, e : e + 1].astype(jnp.int32) + start + e * cap
        at = (wide == slot) & (hits[e] > 0.5)
        chosen = jnp.where(at, 1.0, chosen)
        gain = jnp.where(at, gains[e], gain)
    pick[...] = jnp.transpose(chosen).astype(BF16)
    mix[...] = gain


def half_cols(hid, mine):
    core = lax.axis_index("grp") & 1
    return pl.ds(pl.multiple_of((core if mine else 1 - core) * hid, hid), hid)


def half_products(experts, mine, x, gate, up, out):
    hid = out.shape[2] // 2
    cap = out.shape[1]
    cols = half_cols(hid, mine)
    for i, e in enumerate(experts):
        xe = x[e * cap : (e + 1) * cap]
        for j, w in enumerate((gate, up)):
            v = jnp.dot(xe, w[e, :, cols], preferred_element_type=F32)
            out[i, :, j * hid : (j + 1) * hid] = v.astype(out.dtype)


def first_half_body(experts, pick, gate, up, *refs):
    *parts, x, send = refs
    rows = jnp.concatenate([p[...] for p in parts], 0)
    x[...] = jnp.dot(pick[...], rows, preferred_element_type=F32).astype(BF16)
    half_products(experts, False, x, gate, up, send)


def half_body(experts, mine, x, gate, up, out):
    half_products(experts, mine, x, gate, up, out)


def own_sum_body(experts, x, gate, up, other, keep, send):
    hid = send.shape[2] // 2
    cap = send.shape[1]
    cols = half_cols(hid, True)
    for i, e in enumerate(experts):
        xe = x[e * cap : (e + 1) * cap]
        for j, w in enumerate((gate, up)):
            at = slice(j * hid, (j + 1) * hid)
            v = jnp.dot(xe, w[e, :, cols], preferred_element_type=F32) + other[e, :, at].astype(F32)
            keep[i, :, at] = v
            send[i, :, at] = v.astype(BF16)


def add_body(experts, x, other, keep, send):
    for i, e in enumerate(experts):
        v = x[i] + other[e].astype(F32)
        keep[i] = v
        send[i] = v.astype(BF16)


def act_body(keep, *refs):
    *others, out = refs
    hid = out.shape[2]
    for i in range(out.shape[0]):
        x = keep[i]
        for o in others:
            x = x + o[i].astype(F32)
        gate, up = x[:, :hid], x[:, hid:]
        out[i] = (gate / (1.0 + jnp.exp(-gate)) * up).astype(BF16)


def weigh(mix, result):
    gain = mix[...]
    rows = gain.shape[0]
    hi = gain.astype(BF16)
    lo = (gain - hi.astype(F32)).astype(BF16)
    v = jnp.dot(jnp.concatenate([hi, lo], 0), result, preferred_element_type=F32)
    return v[:rows] + v[rows:]


def down_mine_body(experts, mine, down, out):
    low = half_cols(mine.shape[2], True)
    for i, e in enumerate(experts):
        out[i] = jnp.dot(mine[i], down[e, low], preferred_element_type=F32)


def down_next_body(experts, later, part, other, mine, down, out, ahead):
    low, high = half_cols(mine.shape[2], True), half_cols(mine.shape[2], False)
    for i, e in enumerate(experts):
        v = part[i] + jnp.dot(other[i], down[e, high], preferred_element_type=F32)
        out[i] = v.astype(BF16)
    for i, e in enumerate(later):
        ahead[i] = jnp.dot(mine[i], down[e, low], preferred_element_type=F32)


def down_last_body(n_before, experts, part, other, down, mix, *refs):
    high = half_cols(other.shape[2], False)
    parts = [r[i] for r in refs[:n_before] for i in range(r.shape[0])]
    for i, e in enumerate(experts):
        v = part[i] + jnp.dot(other[i], down[e, high], preferred_element_type=F32)
        parts.append(v.astype(BF16))
    keep, *sends = refs[n_before:]
    v = weigh(mix, jnp.concatenate(parts, 0))
    n = keep.shape[0]
    keep[...] = v[:n]
    for s, send in enumerate(sends, 1):
        send[...] = v[s * n : (s + 1) * n].astype(BF16)


def last_sum_body(keep, *refs):
    *others, own, send = refs
    count = own.shape[0]
    x = keep[...]
    for o in others:
        x = x + o[...].astype(F32)
    own[...] = x[:count]
    send[...] = x[count:].astype(BF16)


def out_body(hidden, own, other, out):
    out[...] = (hidden[...] + own[...] + other[...].astype(F32)).astype(BF16)


def bind(body, *first):
    def bound(*refs):
        return body(*first, *refs)

    return bound


def per_device(
    q_nope, q_rope, w_uk, w_uv, prompt, w_out, residual, routes, route_scores,
    expert_gate, expert_up, expert_down,
):
    rows, heads, nope = q_nope.shape
    lat, vdim = w_uk.shape[2], w_uv.shape[2]
    n_grp, n_ctx = lax.axis_size("grp"), lax.axis_size("ctx")
    count, width = residual.shape
    top = routes.shape[1]
    experts, _, ff = expert_gate.shape
    cap = CAP * n_ctx
    hid = ff // 2
    hv = heads // 2 * vdim
    tail = -(-width // LANES) * LANES
    far = n_ctx // 2
    in_vmem = lambda a: pltpu.with_memory_space_constraint(a, VMEM)

    keys = prompt.T
    far_keys = swap(keys, "grp", 1)
    many = heads // 2 * rows
    queries, turned, keys = run(
        "queries", query_body,
        [((many, lat), BF16), ((many, q_rope.shape[2]), BF16), (keys.shape, BF16)],
        [q_nope, q_rope, w_uk, keys],
        scratch=[
            VMEM(q_nope.shape, BF16), VMEM(q_rope.shape, BF16), VMEM((heads // 2,) + w_uk.shape[1:], BF16),
            VMEM((heads, rows, nope), BF16), VMEM((heads, rows, q_rope.shape[2]), BF16),
            pltpu.SemaphoreType.DMA((3 + max(1, heads // 8),)),
        ],
        us=2, limit=6, hbm=range(4),
    )
    scale = (nope + q_rope.shape[2]) ** (-0.5)
    keep, send = run(
        "attend", bind(attend_body, scale), [((rows, hv + LANES), F32), ((rows, hv + LANES), BF16)],
        [queries, turned, keys, far_keys, w_uv],
        scratch=[
            VMEM((heads // 2,) + w_uv.shape[1:], BF16), VMEM((keys.shape[0], 2 * keys.shape[1]), BF16),
            pltpu.SemaphoreType.DMA((1,)),
        ],
        us=12, limit=12, hbm=(4,),
    )
    (mine,) = run(
        "merge", bind(merge_body, heads // 2), [((rows, hv), BF16)], [keep] + spread(send, "grp"), us=1
    )
    other = swap(mine, "grp", 1)
    w_out = in_vmem(w_out)
    (part,) = run("project_mine", project_mine_body, [((rows, width), F32)], [mine, w_out], us=0.5)
    pair = 2 * count
    keep, *sends, info = run(
        "project", project_body,
        [((pair, width), F32)] + [((pair, tail + LANES), BF16)] * (far - 1) + [((count, LANES), F32)],
        [part, other, routes, route_scores, w_out],
        scratch=[VMEM((rows, width), F32), VMEM((pair, LANES), F32)], us=1,
    )
    wide = -(-32 * far // LANES) * LANES
    own, send = run(
        "rest_sum", bind(rest_sum_body, list(far_first("ctx"))),
        [((pair, width), F32), ((pair, tail + wide), BF16)],
        [keep, residual, info] + scatter(sends, "ctx"), us=1,
    )
    other = swap(send, "ctx", 1)
    hidden, moe = run(
        "hidden", hidden_body, [((count, width), F32), ((pair, width), BF16)], [own, other], us=1
    )
    parts = dict(zip(far_first("ctx"), spread(moe, "ctx")))
    parts[0] = moe
    pick, mix = run(
        "route", bind(route_body, experts, top, tail),
        [((experts * cap, rows), BF16), ((rows, experts * cap), F32)], [send, other], us=0.5, after=[parts[far - 1]],
    )
    gate, up, down = in_vmem(expert_gate), in_vmem(expert_up), in_vmem(expert_down)
    size = -(-experts // 2)
    groups = [range(i, i + size) for i in range(0, experts, size)]
    shape = (size, cap, 2 * hid)
    whole = (experts, cap, 2 * hid)
    x, send = run(
        "other_half", bind(first_half_body, range(experts)),
        [((experts * cap, width), BF16), (whole, BF16)],
        [pick, gate, up] + [parts[s] for s in range(far)], us=0.5,
    )
    other = swap(send, "grp", 1)
    sums = []
    for g in groups:
        if sums:
            keep, send = run(
                "own_sum", bind(own_sum_body, g), [(shape, F32), (shape, BF16)],
                [x, gate, up, other], us=0.5, after=[sums[-1][0]],
            )
        else:
            (part,) = run(
                "own_half", bind(half_body, g, True), [(shape, F32)], [x, gate, up], us=0.5, after=[send]
            )
            keep, send = run(
                "add", bind(add_body, g), [(shape, F32), (shape, BF16)], [part, other], us=0.1
            )
        sums.append((keep, spread(send, "grp")))
    before, later = [], []
    for g, (keep, others) in zip(groups, sums):
        (act,) = run(
            "act", act_body, [((size, cap, hid), BF16)], [keep] + others, us=5,
            after=later or [sums[-1][0]],
        )
        other_act = swap(act, "grp", 1)
        if later:
            before, part = run(
                "down_next", bind(down_next_body, groups[0], g),
                [((size, cap, width), BF16), ((size, cap, width), F32)],
                [later[0], last_act, act, down], us=1,
            )
            before = [before]
        else:
            (part,) = run(
                "down_mine", bind(down_mine_body, g), [((size, cap, width), F32)], [act, down], us=0.5
            )
            later, last_act = [part], other_act
    keep, *sends = run(
        "down_last", bind(down_last_body, len(before), groups[-1]),
        [((pair, width), F32)] + [((pair, width), BF16)] * (far - 1),
        [part, other_act, down, mix] + before, us=1,
    )
    own, send = run(
        "last_sum", last_sum_body, [((count, width), F32), ((count, width), BF16)],
        [keep] + scatter(sends, "ctx"), us=3,
    )
    (out,) = run(
        "out", out_body, [((count, width), BF16)], [hidden, own, swap(send, "ctx", 1)], us=1
    )
    return out


def solution(mesh):
    in_specs = (
        P(None, "ctx", None),
        P(None, "ctx", None),
        P("ctx", None, None),
        P("ctx", None, None),
        P("grp", None),
        P("ctx", "grp"),
        P("ctx", "grp"),
        P("ctx", None),
        P("ctx", None),
        P("ctx", "grp", None),
        P("ctx", "grp", None),
        P("ctx", None, "grp"),
    )
    return jax.shard_map(
        per_device, mesh=mesh, in_specs=in_specs, out_specs=P("ctx", "grp"), check_vma=False
    )
```
